32 devices in a mesh: ctx: 16 (over z, y, x), ch: 2 (over core).
Axes of the slice: x: 2, y: 2, z: 4, core: 2. Of those that a mesh axis runs over, the one named last changes fastest.
Arguments:
- query: bfloat16 [2048, 4096], P('ctx', 'ch'), may hold values from -6 to 6
- key: bfloat16 [2048, 4096], P('ctx', 'ch'), may hold values from -6 to 6
- value: bfloat16 [2048, 4096], P('ctx', 'ch'), may hold values from -6 to 6
- filter_taps: float32 [2048, 256], P('ctx', 'ch'), may hold values from -0.125 to 0.125
- conv_bias: float32 [4096], P('ch'), may hold values from -4 to 4
- norm_gain: float32 [4096], P('ch'), may hold values from 0.1 to 1.9
- pair_list: int32 [136, 3], replicated, may hold values from 0 to 15, as said below
Outputs:
- mixed: bfloat16 [2048, 4096], P('ctx', 'ch')
The draws below stay inside these ranges and needn't reach their ends.
Inputs may be any that keep to these rules, and one draw needn't show every extreme that they name: `pair_list`: every pair of blocks with source <= target appears once, in no particular order. A row with source = target names the device that holds that block; blocks c and 15 - c are held by two devices whose indices differ only in the lowest bit. Every other pair is executed by one of those two devices for its target block. Each device executes at most 9 pairs.
All inputs are finite; a program needn't handle non-finite values.
Results may differ from the reference program's by a relative error of at most 0.0049.
Values may be sent and summed in bfloat16 or wider, within the bound.
A program may use at most 64 MiB of HBM per device.

```python
import jax
import jax.numpy as jnp
import numpy as np
from jax import lax

SPAN = 128
CHANNELS = 4096
GROUP = 16
FILTERS = 256
SEQ = 2048


def draw_pair_list(key, part):
    blocks = SEQ // SPAN
    half_count = blocks // 2
    pair_perm = jax.random.permutation(jax.random.fold_in(key, 1), half_count).astype(jnp.int32)
    flipped = jax.random.randint(jax.random.fold_in(key, 2), (half_count,), 0, 2).astype(jnp.int32)
    short_dev = 2 * pair_perm + flipped
    long_dev = 2 * pair_perm + 1 - flipped
    row_keys = jax.random.split(jax.random.fold_in(key, 3), half_count)
    scores = jax.vmap(lambda k: jax.random.permutation(k, blocks))(row_keys).astype(jnp.int32)
    row_ids = jnp.arange(half_count, dtype=jnp.int32)[:, None]
    sources = jnp.arange(blocks, dtype=jnp.int32)[None, :]
    eligible = sources <= blocks - 2 - row_ids
    smaller = eligible[:, None, :] & (scores[:, None, :] < scores[:, :, None])
    ranked = jnp.sum(smaller.astype(jnp.int32), axis=2)
    chosen = eligible & (ranked < half_count - row_ids)
    target_np, source_np = np.tril_indices(blocks)
    target_all = jnp.asarray(target_np.astype(np.int32))
    source_all = jnp.asarray(source_np.astype(np.int32))
    row_pair = jnp.minimum(target_all, blocks - 1 - target_all)
    is_short = target_all < half_count
    picked = chosen[row_pair, source_all]
    runner = jnp.where(is_short | picked, short_dev[row_pair], long_dev[row_pair])
    rows = jnp.stack([source_all, target_all, runner.astype(jnp.int32)], axis=1).astype(jnp.int32)
    shuffle = jax.random.permutation(jax.random.fold_in(key, 4), rows.shape[0])
    return rows[shuffle]


def level_of(rng, dims, shards, least, largest):
    def one(axis_at, shards_of):
        heights = jax.random.uniform(jax.random.fold_in(jax.random.fold_in(rng, 6), axis_at), (shards_of,), jnp.float32, least / len(shards), largest / len(shards))
        return jnp.repeat(jnp.exp(heights), dims[axis_at] // shards_of).reshape((-1,) + (1,) * (len(dims) - axis_at - 1))

    factor_of = one(*shards[0])
    for cut in shards[1:]:
        factor_of = factor_of * one(*cut)
    return factor_of


def gaussian(key, extent, scale, most, pieces=(), held_as=jnp.bfloat16):
    result = scale * jax.random.normal(key, extent, jnp.float32)
    if pieces:
        result = result * level_of(key, extent, pieces, -0.22, 0.18)
    return jnp.clip(result, -most, most).astype(held_as)


def setup_inputs(seed: int = 0) -> dict:
    seeds = jax.random.split(jax.random.key(seed), 8)
    return {
        "query": gaussian(seeds[0], (SEQ, CHANNELS), 1.0, 6.0, ((0, 16), (1, 2))),
        "key": gaussian(seeds[1], (SEQ, CHANNELS), 1.0, 6.0, ((0, 16), (1, 2))),
        "value": gaussian(seeds[2], (SEQ, CHANNELS), 1.0, 6.0, ((0, 16), (1, 2))),
        "filter_taps": gaussian(seeds[3], (SEQ, FILTERS), SEQ ** -0.5, 0.125, ((0, 16), (1, 2)), jnp.float32),
        "conv_bias": gaussian(seeds[4], (CHANNELS,), 1.0, 4.0, ((0, 2),), jnp.float32),
        "norm_gain": jnp.clip(1.0 + 0.18 * jax.random.normal(seeds[5], (CHANNELS,), jnp.float32), 0.1, 1.9),
        "pair_list": draw_pair_list(jax.random.fold_in(seeds[7], 71), 0),
    }


def reference(query, key, value, filter_taps, conv_bias, norm_gain, pair_list):
    blocks = SEQ // SPAN
    source = pair_list[:, 0]
    target = pair_list[:, 1]
    runner = pair_list[:, 2]
    on_diag = source == target
    slots = jnp.arange(blocks, dtype=jnp.int32)
    holds = on_diag[:, None] & (runner[:, None] == slots[None, :])
    holder = lax.optimization_barrier(jnp.sum(jnp.where(holds, source[:, None], 0), axis=0)).astype(jnp.int32)
    keeps = on_diag[:, None] & (source[:, None] == slots[None, :])
    device_of = lax.optimization_barrier(jnp.sum(jnp.where(keeps, runner[:, None], 0), axis=0)).astype(jnp.int32)
    signal = (key.astype(jnp.float32) * value.astype(jnp.float32)).astype(jnp.bfloat16)
    ordered = signal.astype(jnp.float32).reshape(blocks, SPAN, CHANNELS)[device_of].reshape(SEQ, CHANNELS)
    taps = jnp.repeat(filter_taps, GROUP, axis=1)
    length = 2 * SEQ
    spectrum = jnp.fft.rfft(ordered, n=length, axis=0) * jnp.fft.rfft(taps, n=length, axis=0)
    long_conv = jnp.fft.irfft(spectrum, n=length, axis=0)[:SEQ]
    long_conv = long_conv + conv_bias[None, :] * ordered
    placed = long_conv.reshape(blocks, SPAN, CHANNELS)[holder].reshape(SEQ, CHANNELS)
    gated = query.astype(jnp.float32) * placed
    meansq = lax.optimization_barrier(jnp.mean(gated * gated, axis=1, keepdims=True))
    return (gated * lax.rsqrt(meansq + 1e-05) * norm_gain[None, :]).astype(jnp.bfloat16)
```

```python
import functools

import jax
import jax.numpy as jnp
from jax import lax
from jax.experimental import pallas as pl
from jax.experimental.pallas import tpu as pltpu
from jax.sharding import PartitionSpec as P

MESH = pl.DeviceIdType.MESH
LANES = 128
STRIP = 8
F32 = jnp.float32
BF16 = jnp.bfloat16


class Plan:
    def __init__(self, mesh, channels, filters, rows):
        self.blocks = mesh.shape["ctx"]
        self.halves = mesh.shape["ch"]
        self.rows = rows
        self.channels = channels
        self.filters = filters
        self.group = channels // filters
        self.each = max(1, filters // self.blocks)
        self.workers = filters // self.each
        self.share = self.each * self.group
        self.parts = 2 if self.each % 2 == 0 else 1
        self.each_part = self.each // self.parts
        self.share_part = self.share // self.parts


def kernel(plan, device_of, holder, query, key, value, taps, bias, gain, out, *scratch):
    blocks, rows, group = plan.blocks, plan.rows, plan.group
    share, part_rows = plan.share, plan.share_part
    parts = range(plan.parts)
    scratch = list(scratch)
    take = lambda count: [scratch.pop(0) for _ in range(count)]
    flipped, taps_flipped, taps_got, toeplitz, total, results, gated, squares = take(8)
    got, ordered, made, staged = (take(plan.parts) for _ in range(4))
    taps_send, taps_recv, square_send, square_recv = take(4)
    go_send, go_recv, back_send, back_recv = (take(plan.parts) for _ in range(4))

    me = lax.axis_index("ctx")
    half = lax.axis_index("ch")

    def only_worker(index):
        if plan.workers == blocks:
            return lambda fn: fn()
        return pl.when(index < plan.workers)

    def peer_of(step):
        return lax.rem(me + step, blocks)

    def taps_copy(peer, slot):
        return pltpu.make_async_remote_copy(
            src_ref=taps_flipped.at[peer],
            dst_ref=taps_got.at[slot],
            send_sem=taps_send.at[peer],
            recv_sem=taps_recv.at[slot],
            device_id={"ctx": peer},
            device_id_type=MESH,
        )

    def go_copy(part, peer, slot):
        first = pl.multiple_of(peer * share + part * part_rows, group)
        return pltpu.make_async_remote_copy(
            src_ref=flipped.at[pl.ds(first, part_rows)],
            dst_ref=got[part].at[slot],
            send_sem=go_send[part].at[peer],
            recv_sem=go_recv[part].at[slot],
            device_id={"ctx": peer},
            device_id_type=MESH,
        )

    def back_copy(part, peer, slot):
        first = pl.multiple_of(slot * share + part * part_rows, group)
        return pltpu.make_async_remote_copy(
            src_ref=staged[part].at[peer],
            dst_ref=results.at[pl.ds(first, part_rows)],
            send_sem=back_send[part].at[peer],
            recv_sem=back_recv[part].at[slot],
            device_id={"ctx": peer},
            device_id_type=MESH,
        )

    def square_copy(peer, slot):
        return pltpu.make_async_remote_copy(
            src_ref=squares.at[half],
            dst_ref=squares.at[slot],
            send_sem=square_send.at[peer],
            recv_sem=square_recv.at[slot],
            device_id={"ch": peer},
            device_id_type=MESH,
        )

    barrier = pltpu.get_barrier_semaphore()

    @pl.loop(1, blocks)
    def _(step):
        pl.semaphore_signal(
            barrier, inc=1, device_id={"ctx": peer_of(step)}, device_id_type=MESH
        )

    for step in range(1, plan.halves):
        pl.semaphore_signal(
            barrier,
            inc=1,
            device_id={"ch": lax.rem(half + step, plan.halves)},
            device_id_type=MESH,
        )

    all_taps = jnp.transpose(taps[...])
    if plan.each == STRIP:
        taps_flipped[...] = all_taps.reshape(plan.workers, STRIP, rows)
    else:
        for worker in range(plan.workers):
            for index in range(plan.each):
                row = worker * plan.each + index
                taps_flipped[worker, index : index + 1, :] = all_taps[row : row + 1, :]

    def signal_tile(columns):
        return key[:, columns].astype(F32) * value[:, columns].astype(F32)

    @pl.loop(0, plan.channels // LANES)
    def _(tile):
        at = pl.ds(pl.multiple_of(tile * LANES, LANES), LANES)
        flipped[at, :] = jnp.transpose(signal_tile(at)).astype(BF16)

    pl.semaphore_wait(barrier, blocks - 1 + plan.halves - 1)

    @pl.loop(1, blocks)
    def _(step):
        peer = peer_of(step)

        @only_worker(peer)
        def _():
            taps_copy(peer, me).start()

    for part in parts:

        @pl.loop(1, blocks)
        def _(step, part=part):
            peer = peer_of(step)

            @only_worker(peer)
            def _():
                go_copy(part, peer, me).start()

    @only_worker(me)
    def _():
        taps_got[me] = taps_flipped[me]
        for part in parts:
            first = pl.multiple_of(me * share + part * part_rows, group)
            got[part][me] = flipped[pl.ds(first, part_rows), :]

        @pl.loop(1, blocks)
        def _(step):
            taps_copy(me, peer_of(step)).wait_recv()

        at_row = lax.broadcasted_iota(jnp.int32, (rows, LANES), 0)
        at_lane = lax.broadcasted_iota(jnp.int32, (rows, LANES), 1)
        ahead = at_lane >= at_row

        @pl.loop(0, plan.each)
        def _(index):
            def one(block, before):
                line = taps_got[block, pl.ds(index, 1), :]
                turned = pltpu.roll(
                    jnp.broadcast_to(line, (rows, LANES)), 0, 1, stride=1, stride_axis=0
                )
                at = pl.ds(pl.multiple_of(block * LANES, LANES), LANES)
                toeplitz[index, :, at] = jnp.where(ahead, turned, before).astype(BF16)
                return turned

            lax.fori_loop(0, blocks, one, jnp.zeros((rows, LANES), F32))

        for part in parts:

            @pl.loop(1, blocks)
            def _(step, part=part):
                go_copy(part, me, peer_of(step)).wait_recv()

            @pl.loop(0, blocks)
            def _(block, part=part):
                piece = got[part][device_of[block]]
                at = pl.ds(pl.multiple_of(block * group, group), group)
                for index in range(plan.each_part):
                    ordered[part][index, at, :] = piece[index * group : (index + 1) * group]

            @pl.loop(0, plan.each_part)
            def _(index, part=part):
                for pair in range(blocks // 2):
                    height = (blocks - 2 * pair) * group
                    product = jnp.dot(
                        ordered[part][index, :height, :],
                        toeplitz[
                            part * plan.each_part + index,
                            :,
                            2 * pair * LANES : 2 * (pair + 1) * LANES,
                        ],
                        preferred_element_type=F32,
                    )
                    even, odd = 2 * pair * group, (2 * pair + 1) * group
                    if pair == 0:
                        total[...] = product[:, :LANES]
                    else:
                        total[even:, :] += product[:, :LANES]
                    total[odd:, :] += product[: height - group, LANES:]
                at = pl.ds(pl.multiple_of(index * group, group), group)
                made[part][:, at, :] = total[...].astype(BF16).reshape(blocks, group, LANES)

            @pl.loop(1, blocks)
            def _(step, part=part):
                peer = peer_of(step)
                staged[part][peer] = made[part][holder[peer]]
                back_copy(part, peer, me).start()

            first = pl.multiple_of(me * share + part * part_rows, group)
            results[pl.ds(first, part_rows), :] = made[part][holder[me]]

    per_tile = LANES // share if share < LANES else 1
    tiles_each = share // LANES if share > LANES else 1

    def finish(tile, sums):
        for near in range(per_tile):
            worker = tile * per_tile + near if tiles_each == 1 else tile // tiles_each

            def wait(worker=worker):
                @pl.when(worker != me)
                def _():
                    for part in parts:
                        back_copy(part, me, worker).wait_recv()

            if tiles_each == 1:
                wait()
            else:
                pl.when(lax.rem(tile, tiles_each) == 0)(wait)
        at = pl.ds(pl.multiple_of(tile * LANES, LANES), LANES)
        conv = jnp.transpose(results[at, :].astype(F32))
        signal = signal_tile(at).astype(BF16).astype(F32)
        product = query[:, at].astype(F32) * (conv + bias[:, at] * signal)
        gated[:, at] = product
        return sums + product * product

    tiles = plan.channels // LANES
    sums = lax.fori_loop(0, tiles, finish, jnp.zeros((rows, LANES), F32))
    squares[half] = jnp.broadcast_to(jnp.sum(sums, axis=1, keepdims=True), (rows, LANES))
    for step in range(1, plan.halves):
        square_copy(lax.rem(half + step, plan.halves), half).start()
    for step in range(1, plan.halves):
        square_copy(half, lax.rem(half + step, plan.halves)).wait_recv()
    whole = squares[0]
    for other in range(1, plan.halves):
        whole = whole + squares[other]
    scaling = lax.rsqrt(whole / (plan.channels * plan.halves) + 1e-05)

    @pl.loop(0, tiles)
    def _(tile):
        at = pl.ds(pl.multiple_of(tile * LANES, LANES), LANES)
        out[:, at] = (gated[:, at] * scaling * gain[:, at]).astype(BF16)

    for step in range(1, plan.halves):
        square_copy(lax.rem(half + step, plan.halves), half).wait_send()

    @pl.loop(1, blocks)
    def _(step):
        peer = peer_of(step)

        @only_worker(peer)
        def _():
            taps_copy(peer, me).wait_send()
            for part in parts:
                go_copy(part, peer, me).wait_send()

        @only_worker(me)
        def _():
            for part in parts:
                back_copy(part, peer, me).wait_send()


def body(mesh, query, key, value, filter_taps, conv_bias, norm_gain, pair_list):
    rows, channels = query.shape
    plan = Plan(mesh, channels, filter_taps.shape[1], rows)
    blocks, parts = plan.blocks, plan.parts
    source, target, runner = pair_list[:, 0], pair_list[:, 1], pair_list[:, 2]
    slots = lax.iota(jnp.int32, blocks)
    on_diag = (source == target)[:, None]
    keeps = on_diag & (source[:, None] == slots[None, :])
    holds = on_diag & (runner[:, None] == slots[None, :])
    device_of = jnp.sum(jnp.where(keeps, runner[:, None], 0), axis=0)
    holder = jnp.sum(jnp.where(holds, source[:, None], 0), axis=0)

    vmem = pl.BlockSpec(memory_space=pltpu.VMEM)
    smem = pl.BlockSpec(memory_space=pltpu.SMEM)
    strip = max(STRIP, plan.each)
    part_piece = (blocks, plan.share_part, LANES)
    sems = pltpu.SemaphoreType.DMA
    scratch = [
        pltpu.VMEM((channels, LANES), BF16),
        pltpu.VMEM((blocks, strip, LANES), F32),
        pltpu.VMEM((blocks, strip, LANES), F32),
        pltpu.VMEM((plan.each, rows, blocks * LANES), BF16),
        pltpu.VMEM((blocks * plan.group, LANES), F32),
        pltpu.VMEM((channels, LANES), BF16),
        pltpu.VMEM((rows, channels), F32),
        pltpu.VMEM((plan.halves, rows, LANES), F32),
    ]
    scratch += [pltpu.VMEM(part_piece, BF16)] * parts
    scratch += [pltpu.VMEM((plan.each_part, blocks * plan.group, LANES), BF16)] * parts
    scratch += [pltpu.VMEM(part_piece, BF16)] * parts
    scratch += [pltpu.VMEM(part_piece, BF16)] * parts
    scratch += [sems((blocks,)), sems((blocks,)), sems((plan.halves,)), sems((plan.halves,))]
    scratch += [sems((blocks,))] * (4 * parts)
    pairs = blocks * (blocks + 2) // 4
    return pl.pallas_call(
        functools.partial(kernel, plan),
        out_shape=jax.ShapeDtypeStruct((rows, channels), BF16),
        in_specs=[smem, smem] + [vmem] * 6,
        out_specs=vmem,
        scratch_shapes=scratch,
        compiler_params=pltpu.CompilerParams(
            collective_id=0, has_side_effects=True, vmem_limit_bytes=48 * 1024 * 1024
        ),
        cost_estimate=pl.CostEstimate(
            flops=2 * plan.each * pairs * plan.group * rows * 2 * LANES,
            bytes_accessed=8 * rows * channels,
            transcendentals=0,
        ),
    )(
        device_of.astype(jnp.int32),
        holder.astype(jnp.int32),
        query,
        key,
        value,
        filter_taps,
        conv_bias[None, :],
        norm_gain[None, :],
    )


def solution(mesh):
    placed = (P("ctx", "ch"), P("ctx", "ch"), P("ctx", "ch"), P("ctx", "ch"), P("ch"), P("ch"), P())
    return jax.shard_map(
        functools.partial(body, mesh),
        mesh=mesh,
        in_specs=placed,
        out_specs=P("ctx", "ch"),
        check_vma=False,
    )
```

```python
import functools

import jax
import jax.numpy as jnp
from jax import lax
from jax.experimental import pallas as pl
from jax.experimental.pallas import tpu as pltpu
from jax.sharding import PartitionSpec as P

MESH = pl.DeviceIdType.MESH
LANES = 128
VMEM_BYTES = 63 * 1024 * 1024
STRIP = 8
F32 = jnp.float32
BF16 = jnp.bfloat16


class Plan:
    def __init__(self, mesh, channels, filters, rows):
        self.blocks = mesh.shape["ctx"]
        self.halves = mesh.shape["ch"]
        self.rows = rows
        self.channels = channels
        self.filters = filters
        self.group = channels // filters
        self.each = max(1, filters // self.blocks)
        self.workers = filters // self.each
        self.share = self.each * self.group
        self.parts = 4 if self.each % 4 == 0 else 1
        self.each_part = self.each // self.parts
        self.share_part = self.share // self.parts
        self.span = channels // self.parts


def kernel(plan, pairs, query, key, value, taps, bias, gated_out, scale, *scratch):
    blocks, rows, group, span = plan.blocks, plan.rows, plan.group, plan.span
    part_rows = plan.share_part
    parts = range(plan.parts)
    scratch = list(scratch)
    take = lambda count: [scratch.pop(0) for _ in range(count)]
    pairs_here, table, table_here, query_here, key_here, value_here, taps_here, bias_here = take(8)
    (gated,) = take(1)
    flipped, taps_rows, taps_flipped, taps_got, toeplitz, total, results, squares = take(8)
    got, ordered, made, staged = (take(plan.parts) for _ in range(4))
    taps_send, taps_recv, square_send, square_recv, loaded, loaded_part = take(6)
    (stored,) = take(1)
    go_send, go_recv, back_send, back_recv = (take(plan.parts) for _ in range(4))

    me = lax.axis_index("ctx")
    half = lax.axis_index("ch")

    def only_worker(index):
        if plan.workers == blocks:
            return lambda fn: fn()
        return pl.when(index < plan.workers)

    def slot_of(step):
        return lax.rem(me + step, blocks)

    bits = [1 << place for place in range((blocks - 1).bit_length())]
    digits = [lax.rem(lax.div(me, bit), 2) for bit in bits]

    def peer_of(mask):
        peer = me
        for bit, digit in zip(bits, digits):
            flip = (mask // bit) % 2 if isinstance(mask, int) else lax.rem(lax.div(mask, bit), 2)
            peer = peer + flip * bit * (1 - 2 * digit)
        return peer

    near = [peer_of(blocks - step) for step in range(1, blocks)] if blocks <= 16 else None

    def each_peer(act):
        if near is not None:
            for peer in near:
                act(peer)
        else:
            pl.loop(1, blocks)(lambda step: act(peer_of(blocks - step)))

    def column_copies(part):
        at = pl.ds(part * span, span)
        return [
            pltpu.make_async_copy(there.at[:, at], here.at[:, at], loaded_part.at[part, place])
            for place, (there, here) in enumerate(((key, key_here), (value, value_here)))
        ]

    def gated_store(part):
        at = pl.ds(part * span, span)
        return pltpu.make_async_copy(gated.at[:, at], gated_out.at[:, at], stored.at[part])

    whole_copies = [
        pltpu.make_async_copy(there, here, loaded.at[place])
        for place, (there, here) in enumerate(
            ((taps, taps_here), (pairs, pairs_here), (bias, bias_here), (query, query_here))
        )
    ]
    taps_load, pairs_load, bias_load, query_load = whole_copies
    table_load = pltpu.make_async_copy(table, table_here, loaded.at[4])

    def taps_copy(peer, slot):
        return pltpu.make_async_remote_copy(
            src_ref=taps_flipped.at[peer],
            dst_ref=taps_got.at[slot],
            send_sem=taps_send.at[peer],
            recv_sem=taps_recv.at[slot],
            device_id={"ctx": peer},
            device_id_type=MESH,
        )

    def go_copy(part, peer, slot):
        first = pl.multiple_of(part * span + peer * part_rows, group)
        return pltpu.make_async_remote_copy(
            src_ref=flipped.at[pl.ds(first, part_rows)],
            dst_ref=got[part].at[slot],
            send_sem=go_send[part].at[peer],
            recv_sem=go_recv[part].at[slot],
            device_id={"ctx": peer},
            device_id_type=MESH,
        )

    def back_copy(part, peer, slot):
        first = pl.multiple_of(part * span + slot * part_rows, group)
        return pltpu.make_async_remote_copy(
            src_ref=staged[part].at[peer],
            dst_ref=results.at[pl.ds(first, part_rows)],
            send_sem=back_send[part].at[peer],
            recv_sem=back_recv[part].at[slot],
            device_id={"ctx": peer},
            device_id_type=MESH,
        )

    def square_copy(peer, slot):
        return pltpu.make_async_remote_copy(
            src_ref=squares.at[half],
            dst_ref=squares.at[slot],
            send_sem=square_send.at[peer],
            recv_sem=square_recv.at[slot],
            device_id={"ch": peer},
            device_id_type=MESH,
        )

    barrier = pltpu.get_barrier_semaphore()

    @each_peer
    def _(peer):
        pl.semaphore_signal(barrier, inc=1, device_id={"ctx": peer}, device_id_type=MESH)

    for step in range(1, plan.halves):
        pl.semaphore_signal(
            barrier,
            inc=1,
            device_id={"ch": lax.rem(half + step, plan.halves)},
            device_id_type=MESH,
        )

    taps_load.start()
    for part in parts:
        for copy in column_copies(part):
            copy.start()
    for copy in (pairs_load, bias_load, query_load):
        copy.start()

    taps_load.wait()
    taps_rows[...] = jnp.transpose(taps_here[...])

    @pl.loop(0, plan.workers)
    def _(worker):
        for part in parts:
            for index in range(plan.each_part):
                row = part * (plan.filters // plan.parts) + worker * plan.each_part + index
                place = part * plan.each_part + index
                taps_flipped[worker, place : place + 1, :] = taps_rows[pl.ds(row, 1), :]

    def signal_tile(columns):
        return key_here[:, columns].astype(F32) * value_here[:, columns].astype(F32)

    part_tiles = span // LANES

    for part in parts:
        for copy in column_copies(part):
            copy.wait()

        @pl.loop(part * part_tiles, (part + 1) * part_tiles)
        def _(tile):
            at = pl.ds(pl.multiple_of(tile * LANES, LANES), LANES)
            flipped[at, :] = jnp.transpose(signal_tile(at)).astype(BF16)

        if part == 0:
            pl.semaphore_wait(barrier, blocks - 1 + plan.halves - 1)

            @each_peer
            def _(peer):
                @only_worker(peer)
                def _():
                    taps_copy(peer, me).start()

        @each_peer
        def _(peer, part=part):
            @only_worker(peer)
            def _():
                go_copy(part, peer, me).start()

    pairs_load.wait()
    source, target, runner = (pairs_here[place : place + 1, :] for place in range(3))
    slots = lax.broadcasted_iota(jnp.int32, (blocks, pairs_here.shape[1]), 0)
    diagonal = source == target
    device_of = jnp.where(diagonal & (source == slots), runner, 0)
    holder = jnp.where(diagonal & (runner == slots), source, 0)
    for place, found in enumerate((device_of, holder)):
        table[place * blocks : (place + 1) * blocks, :] = jnp.broadcast_to(
            jnp.sum(found, axis=1, keepdims=True), (blocks, LANES)
        )
    table_load.start()
    table_load.wait()

    @only_worker(me)
    def _():
        taps_got[me] = taps_flipped[me]
        for part in parts:
            first = pl.multiple_of(part * span + me * part_rows, group)
            got[part][me] = flipped[pl.ds(first, part_rows), :]

        @pl.loop(1, blocks)
        def _(step):
            taps_copy(me, slot_of(step)).wait_recv()

        at_row = lax.broadcasted_iota(jnp.int32, (rows, LANES), 0)
        at_lane = lax.broadcasted_iota(jnp.int32, (rows, LANES), 1)
        ahead = at_lane >= at_row

        for part in parts:

            @pl.loop(part * plan.each_part, (part + 1) * plan.each_part)
            def _(index):
                def one(block, before):
                    line = taps_got[block, pl.ds(index, 1), :]
                    turned = pltpu.roll(
                        jnp.broadcast_to(line, (rows, LANES)), 0, 1, stride=1, stride_axis=0
                    )
                    at = pl.ds(pl.multiple_of(block * LANES, LANES), LANES)
                    toeplitz[index, :, at] = jnp.where(ahead, turned, before).astype(BF16)
                    return turned

                lax.fori_loop(0, blocks, one, jnp.zeros((rows, LANES), F32))

            @pl.loop(1, blocks)
            def _(step, part=part):
                go_copy(part, me, slot_of(step)).wait_recv()

            @pl.loop(0, blocks)
            def _(block, part=part):
                piece = got[part][table_here[block, 0]]
                at = pl.ds(pl.multiple_of(block * group, group), group)
                for index in range(plan.each_part):
                    ordered[part][index, at, :] = piece[index * group : (index + 1) * group]

            @pl.loop(0, plan.each_part)
            def _(index, part=part):
                for pair in range(blocks // 2):
                    height = (blocks - 2 * pair) * group
                    product = jnp.dot(
                        ordered[part][index, :height, :],
                        toeplitz[
                            part * plan.each_part + index,
                            :,
                            2 * pair * LANES : 2 * (pair + 1) * LANES,
                        ],
                        preferred_element_type=F32,
                    )
                    even, odd = 2 * pair * group, (2 * pair + 1) * group
                    if pair == 0:
                        total[...] = product[:, :LANES]
                    else:
                        total[even:, :] += product[:, :LANES]
                    total[odd:, :] += product[: height - group, LANES:]
                at = pl.ds(pl.multiple_of(index * group, group), group)
                made[part][:, at, :] = total[...].astype(BF16).reshape(blocks, group, LANES)

            @each_peer
            def _(peer, part=part):
                staged[part][peer] = made[part][table_here[blocks + peer, 0]]
                back_copy(part, peer, me).start()

            first = pl.multiple_of(part * span + me * part_rows, group)
            results[pl.ds(first, part_rows), :] = made[part][table_here[blocks + me, 0]]

    bias_load.wait()
    query_load.wait()
    per_tile = max(1, LANES // part_rows)
    sums = jnp.zeros((rows, LANES), F32)
    for part in parts:

        def finish(tile, sums, part=part):
            near_tile = tile - part * part_tiles
            for place in range(per_tile):
                worker = lax.div(near_tile * LANES, part_rows) + place

                @pl.when(worker != me)
                def _():
                    back_copy(part, me, worker).wait_recv()

            at = pl.ds(pl.multiple_of(tile * LANES, LANES), LANES)
            conv = jnp.transpose(results[at, :].astype(F32))
            signal = signal_tile(at).astype(BF16).astype(F32)
            product = query_here[:, at].astype(F32) * (conv + bias_here[:, at] * signal)
            gated[:, at] = product
            return sums + product * product

        sums = lax.fori_loop(part * part_tiles, (part + 1) * part_tiles, finish, sums)
        gated_store(part).start()
    squares[half] = jnp.broadcast_to(jnp.sum(sums, axis=1, keepdims=True), (rows, LANES))
    for step in range(1, plan.halves):
        square_copy(lax.rem(half + step, plan.halves), half).start()

    @each_peer
    def _(peer):
        @only_worker(peer)
        def _():
            taps_copy(peer, me).wait_send()
            for part in parts:
                go_copy(part, peer, me).wait_send()

        @only_worker(me)
        def _():
            for part in parts:
                back_copy(part, peer, me).wait_send()

    for step in range(1, plan.halves):
        square_copy(half, lax.rem(half + step, plan.halves)).wait_recv()
    whole = squares[0]
    for other in range(1, plan.halves):
        whole = whole + squares[other]
    scale[...] = lax.rsqrt(whole / (plan.channels * plan.halves) + 1e-05)
    for part in parts:
        gated_store(part).wait()
    for step in range(1, plan.halves):
        square_copy(lax.rem(half + step, plan.halves), half).wait_send()


def body(mesh, query, key, value, filter_taps, conv_bias, norm_gain, pair_list):
    rows, channels = query.shape
    plan = Plan(mesh, channels, filter_taps.shape[1], rows)
    blocks, parts = plan.blocks, plan.parts
    vmem = pl.BlockSpec(memory_space=pltpu.VMEM)
    hbm = pl.BlockSpec(memory_space=pltpu.HBM)
    strip = max(STRIP, plan.each)
    part_piece = (blocks, plan.share_part, LANES)
    sems = pltpu.SemaphoreType.DMA
    scratch = [
        pltpu.VMEM(pair_list.shape[::-1], jnp.int32),
        pltpu.VMEM((2 * blocks, LANES), jnp.int32),
        pltpu.SMEM((2 * blocks, LANES), jnp.int32),
        pltpu.VMEM((rows, channels), BF16),
        pltpu.VMEM((rows, channels), BF16),
        pltpu.VMEM((rows, channels), BF16),
        pltpu.VMEM(filter_taps.shape, F32),
        pltpu.VMEM((1, channels), F32),
        pltpu.VMEM((rows, channels), F32),
        pltpu.VMEM((channels, LANES), BF16),
        pltpu.VMEM((plan.filters, LANES), F32),
        pltpu.VMEM((blocks, strip, LANES), F32),
        pltpu.VMEM((blocks, strip, LANES), F32),
        pltpu.VMEM((plan.each, rows, blocks * LANES), BF16),
        pltpu.VMEM((blocks * plan.group, LANES), F32),
        pltpu.VMEM((channels, LANES), BF16),
        pltpu.VMEM((plan.halves, rows, LANES), F32),
    ]
    scratch += [pltpu.VMEM(part_piece, BF16)] * parts
    scratch += [pltpu.VMEM((plan.each_part, blocks * plan.group, LANES), BF16)] * parts
    scratch += [pltpu.VMEM(part_piece, BF16)] * parts
    scratch += [pltpu.VMEM(part_piece, BF16)] * parts
    scratch += [sems((blocks,)), sems((blocks,)), sems((plan.halves,)), sems((plan.halves,))]
    scratch += [sems((5,)), sems((parts, 2)), sems((parts,))]
    scratch += [sems((blocks,))] * (4 * parts)
    pairs = blocks * (blocks + 2) // 4
    gated, scale = pl.pallas_call(
        functools.partial(kernel, plan),
        out_shape=(
            jax.ShapeDtypeStruct((rows, channels), F32),
            jax.ShapeDtypeStruct((rows, LANES), F32),
        ),
        in_specs=[hbm] * 6,
        out_specs=(hbm, vmem),
        scratch_shapes=scratch,
        compiler_params=pltpu.CompilerParams(
            collective_id=0, has_side_effects=True, vmem_limit_bytes=VMEM_BYTES
        ),
        cost_estimate=pl.CostEstimate(
            flops=2 * plan.each * pairs * plan.group * rows * 2 * LANES,
            bytes_accessed=8 * rows * channels,
            transcendentals=0,
        ),
    )(pair_list.T, query, key, value, filter_taps, conv_bias[None, :])
    return (gated * scale[:, :1] * norm_gain[None, :]).astype(BF16)


def solution(mesh):
    placed = (P("ctx", "ch"), P("ctx", "ch"), P("ctx", "ch"), P("ctx", "ch"), P("ch"), P("ch"), P())
    return jax.shard_map(
        functools.partial(body, mesh),
        mesh=mesh,
        in_specs=placed,
        out_specs=P("ctx", "ch"),
        check_vma=False,
    )
```

```python
import functools

import jax
import jax.numpy as jnp
from jax import lax
from jax.experimental import pallas as pl
from jax.experimental.pallas import tpu as pltpu
from jax.sharding import PartitionSpec as P

MESH = pl.DeviceIdType.MESH
LANES = 128
VMEM_BYTES = 1013 * 64 * 1024
STRIP = 8
F32 = jnp.float32
BF16 = jnp.bfloat16


class Plan:
    def __init__(self, mesh, channels, filters, rows):
        self.blocks = mesh.shape["ctx"]
        self.halves = mesh.shape["ch"]
        self.rows = rows
        self.channels = channels
        self.filters = filters
        self.group = channels // filters
        self.each = max(1, filters // self.blocks)
        self.workers = filters // self.each
        self.share = self.each * self.group
        self.parts = 4 if self.each % 4 == 0 else 1
        self.each_part = self.each // self.parts
        self.share_part = self.share // self.parts
        self.span = channels // self.parts


def kernel(plan, pairs, query, key, value, taps, bias, gain, out, *scratch):
    blocks, rows, group, span = plan.blocks, plan.rows, plan.group, plan.span
    part_rows = plan.share_part
    parts = range(plan.parts)
    scratch = list(scratch)
    take = lambda count: [scratch.pop(0) for _ in range(count)]
    pairs_here, table, table_here, query_here, key_here, value_here, taps_here, bias_here = take(8)
    gain_here, gated = take(2)
    flipped, taps_rows, taps_flipped, taps_got, toeplitz, total, results, squares = take(8)
    got, ordered, made, staged = (take(plan.parts) for _ in range(4))
    taps_send, taps_recv, square_send, square_recv, loaded, loaded_part = take(6)
    go_send, go_recv, back_send, back_recv = take(4)

    me = lax.axis_index("ctx")
    half = lax.axis_index("ch")

    def only_worker(index):
        if plan.workers == blocks:
            return lambda fn: fn()
        return pl.when(index < plan.workers)

    def slot_of(step):
        return lax.rem(me + step, blocks)

    bits = [1 << place for place in range((blocks - 1).bit_length())]
    digits = [lax.rem(lax.div(me, bit), 2) for bit in bits]

    def peer_of(mask):
        peer = me
        for bit, digit in zip(bits, digits):
            flip = (mask // bit) % 2 if isinstance(mask, int) else lax.rem(lax.div(mask, bit), 2)
            peer = peer + flip * bit * (1 - 2 * digit)
        return peer

    near = [peer_of(blocks - step) for step in range(1, blocks)] if blocks <= 16 else None

    def each_peer(act):
        if near is not None:
            for peer in near:
                act(peer)
        else:
            pl.loop(1, blocks)(lambda step: act(peer_of(blocks - step)))

    def column_copies(part):
        at = pl.ds(part * span, span)
        return [
            pltpu.make_async_copy(there.at[:, at], here.at[:, at], loaded_part.at[part, place])
            for place, (there, here) in enumerate(((key, key_here), (value, value_here)))
        ]

    whole_copies = [
        pltpu.make_async_copy(there, here, loaded.at[place])
        for place, (there, here) in enumerate(
            ((taps, taps_here), (pairs, pairs_here), (bias, bias_here), (query, query_here), (gain, gain_here))
        )
    ]
    taps_load, pairs_load, bias_load, query_load, gain_load = whole_copies
    table_load = pltpu.make_async_copy(table, table_here, loaded.at[5])

    strip = taps_flipped.shape[0] // plan.workers

    def strip_of(index):
        return pl.ds(pl.multiple_of(index * strip, strip), strip)

    def arrived(ref, sem):
        pltpu.make_async_remote_copy(
            src_ref=ref,
            dst_ref=ref,
            send_sem=sem,
            recv_sem=sem,
            device_id={"ctx": slot_of(1)},
            device_id_type=MESH,
        ).wait_recv()

    def from_others(wait):
        if plan.workers == blocks:
            wait(blocks - 1)
        else:
            pl.when(me < plan.workers)(lambda: wait(plan.workers - 1))
            pl.when(me >= plan.workers)(lambda: wait(plan.workers))

    def taps_copy(peer, slot):
        return pltpu.make_async_remote_copy(
            src_ref=taps_flipped.at[strip_of(peer)],
            dst_ref=taps_got.at[strip_of(slot)],
            send_sem=taps_send.at[0],
            recv_sem=taps_recv.at[0],
            device_id={"ctx": peer},
            device_id_type=MESH,
        )

    def go_copy(part, peer, slot):
        first = pl.multiple_of(part * span + peer * part_rows, group)
        return pltpu.make_async_remote_copy(
            src_ref=flipped.at[pl.ds(first, part_rows)],
            dst_ref=got[part].at[slot],
            send_sem=go_send.at[part],
            recv_sem=go_recv.at[part],
            device_id={"ctx": peer},
            device_id_type=MESH,
        )

    def back_copy(part, peer, slot):
        first = pl.multiple_of(part * span + slot * part_rows, group)
        return pltpu.make_async_remote_copy(
            src_ref=staged[part].at[peer],
            dst_ref=results.at[pl.ds(first, part_rows)],
            send_sem=back_send.at[part],
            recv_sem=back_recv.at[part],
            device_id={"ctx": peer},
            device_id_type=MESH,
        )

    def square_copy(peer, slot):
        return pltpu.make_async_remote_copy(
            src_ref=squares.at[half],
            dst_ref=squares.at[slot],
            send_sem=square_send.at[peer],
            recv_sem=square_recv.at[slot],
            device_id={"ch": peer},
            device_id_type=MESH,
        )

    barrier = pltpu.get_barrier_semaphore()

    @each_peer
    def _(peer):
        pl.semaphore_signal(barrier, inc=1, device_id={"ctx": peer}, device_id_type=MESH)

    for step in range(1, plan.halves):
        pl.semaphore_signal(
            barrier,
            inc=1,
            device_id={"ch": lax.rem(half + step, plan.halves)},
            device_id_type=MESH,
        )

    taps_load.start()
    for part in parts:
        for copy in column_copies(part):
            copy.start()
    for copy in (pairs_load, bias_load, query_load, gain_load):
        copy.start()

    taps_load.wait()
    taps_rows[...] = jnp.transpose(taps_here[...])

    for part in parts:
        for index in range(plan.each_part):
            row = part * (plan.filters // plan.parts) + index
            taps_flipped[pl.ds(part * plan.each_part + index, plan.workers, stride=strip), :] = (
                taps_rows[pl.ds(row, plan.workers, stride=plan.each_part), :]
            )

    def signal_tile(columns):
        return key_here[:, columns].astype(F32) * value_here[:, columns].astype(F32)

    part_tiles = span // LANES

    for part in parts:
        for copy in column_copies(part):
            copy.wait()

        @pl.loop(part * part_tiles, (part + 1) * part_tiles)
        def _(tile):
            at = pl.ds(pl.multiple_of(tile * LANES, LANES), LANES)
            flipped[at, :] = jnp.transpose(signal_tile(at)).astype(BF16)

        if part == 0:
            pl.semaphore_wait(barrier, blocks - 1 + plan.halves - 1)

            @each_peer
            def _(peer):
                @only_worker(peer)
                def _():
                    taps_copy(peer, me).start()

        @each_peer
        def _(peer, part=part):
            @only_worker(peer)
            def _():
                go_copy(part, peer, me).start()

    pairs_load.wait()
    source, target, runner = (pairs_here[place : place + 1, :] for place in range(3))
    slots = lax.broadcasted_iota(jnp.int32, (blocks, pairs_here.shape[1]), 0)
    diagonal = source == target
    device_of = jnp.where(diagonal & (source == slots), runner, 0)
    holder = jnp.where(diagonal & (runner == slots), source, 0)
    for place, found in enumerate((device_of, holder)):
        table[place * blocks : (place + 1) * blocks, :] = jnp.broadcast_to(
            jnp.sum(found, axis=1, keepdims=True), (blocks, LANES)
        )
    table_load.start()
    table_load.wait()

    @only_worker(me)
    def _():
        taps_got[strip_of(me), :] = taps_flipped[strip_of(me), :]
        for part in parts:
            first = pl.multiple_of(part * span + me * part_rows, group)
            got[part][me] = flipped[pl.ds(first, part_rows), :]

        arrived(taps_got.at[pl.ds(0, (blocks - 1) * strip)], taps_recv.at[0])

        at_row = lax.broadcasted_iota(jnp.int32, (rows, LANES), 0)
        at_lane = lax.broadcasted_iota(jnp.int32, (rows, LANES), 1)
        ahead = at_lane >= at_row

        for part in parts:

            @pl.loop(part * plan.each_part, (part + 1) * plan.each_part)
            def _(index):
                def one(block, before):
                    line = taps_got[pl.ds(block * strip + index, 1), :]
                    turned = pltpu.roll(
                        jnp.broadcast_to(line, (rows, LANES)), 0, 1, stride=1, stride_axis=0
                    )
                    at = pl.ds(pl.multiple_of(block * LANES, LANES), LANES)
                    toeplitz[index, :, at] = jnp.where(ahead, turned, before).astype(BF16)
                    return turned

                lax.fori_loop(0, blocks, one, jnp.zeros((rows, LANES), F32))

            arrived(got[part].at[pl.ds(0, blocks - 1)], go_recv.at[part])

            @pl.loop(0, blocks)
            def _(block, part=part):
                piece = got[part][table_here[block, 0]]
                at = pl.ds(pl.multiple_of(block * group, group), group)
                for index in range(plan.each_part):
                    ordered[part][index, at, :] = piece[index * group : (index + 1) * group]

            @pl.loop(0, plan.each_part)
            def _(index, part=part):
                for pair in range(blocks // 2):
                    height = (blocks - 2 * pair) * group
                    product = jnp.dot(
                        ordered[part][index, :height, :],
                        toeplitz[
                            part * plan.each_part + index,
                            :,
                            2 * pair * LANES : 2 * (pair + 1) * LANES,
                        ],
                        preferred_element_type=F32,
                    )
                    even, odd = 2 * pair * group, (2 * pair + 1) * group
                    if pair == 0:
                        total[...] = product[:, :LANES]
                    else:
                        total[even:, :] += product[:, :LANES]
                    total[odd:, :] += product[: height - group, LANES:]
                at = pl.ds(pl.multiple_of(index * group, group), group)
                made[part][:, at, :] = total[...].astype(BF16).reshape(blocks, group, LANES)

            @each_peer
            def _(peer, part=part):
                staged[part][peer] = made[part][table_here[blocks + peer, 0]]
                back_copy(part, peer, me).start()

            first = pl.multiple_of(part * span + me * part_rows, group)
            results[pl.ds(first, part_rows), :] = made[part][table_here[blocks + me, 0]]

    bias_load.wait()
    query_load.wait()
    sums = jnp.zeros((rows, LANES), F32)
    for part in parts:

        from_others(
            lambda count, part=part: arrived(
                results.at[pl.ds(part * span, count * part_rows)], back_recv.at[part]
            )
        )

        def finish(tile, sums):
            at = pl.ds(pl.multiple_of(tile * LANES, LANES), LANES)
            conv = jnp.transpose(results[at, :].astype(F32))
            signal = signal_tile(at).astype(BF16).astype(F32)
            product = query_here[:, at].astype(F32) * (conv + bias_here[:, at] * signal)
            gated[:, at] = product
            return sums + product * product

        sums = lax.fori_loop(part * part_tiles, (part + 1) * part_tiles, finish, sums)
    squares[half] = jnp.broadcast_to(jnp.sum(sums, axis=1, keepdims=True), (rows, LANES))
    for step in range(1, plan.halves):
        square_copy(lax.rem(half + step, plan.halves), half).start()

    from_others(
        lambda count: arrived(taps_flipped.at[pl.ds(0, count * strip)], taps_send.at[0])
    )
    for part in parts:
        from_others(
            lambda count, part=part: arrived(
                flipped.at[pl.ds(part * span, count * part_rows)], go_send.at[part]
            )
        )

    @only_worker(me)
    def _():
        for part in parts:
            arrived(staged[part].at[pl.ds(0, blocks - 1)], back_send.at[part])

    for step in range(1, plan.halves):
        square_copy(half, lax.rem(half + step, plan.halves)).wait_recv()
    whole = squares[0]
    for other in range(1, plan.halves):
        whole = whole + squares[other]
    scaling = lax.rsqrt(whole / (plan.channels * plan.halves) + 1e-05)
    gain_load.wait()

    @pl.loop(0, plan.channels // LANES)
    def _(tile):
        at = pl.ds(pl.multiple_of(tile * LANES, LANES), LANES)
        out[:, at] = (gated[:, at] * scaling * gain_here[:, at]).astype(BF16)

    for step in range(1, plan.halves):
        square_copy(lax.rem(half + step, plan.halves), half).wait_send()


def body(mesh, query, key, value, filter_taps, conv_bias, norm_gain, pair_list):
    rows, channels = query.shape
    plan = Plan(mesh, channels, filter_taps.shape[1], rows)
    blocks, parts = plan.blocks, plan.parts
    vmem = pl.BlockSpec(memory_space=pltpu.VMEM)
    hbm = pl.BlockSpec(memory_space=pltpu.HBM)
    strip = max(STRIP, plan.each)
    part_piece = (blocks, plan.share_part, LANES)
    sems = pltpu.SemaphoreType.DMA
    scratch = [
        pltpu.VMEM(pair_list.shape[::-1], jnp.int32),
        pltpu.VMEM((2 * blocks, LANES), jnp.int32),
        pltpu.SMEM((2 * blocks, LANES), jnp.int32),
        pltpu.VMEM((rows, channels), BF16),
        pltpu.VMEM((rows, channels), BF16),
        pltpu.VMEM((rows, channels), BF16),
        pltpu.VMEM(filter_taps.shape, F32),
        pltpu.VMEM((1, channels), F32),
        pltpu.VMEM((1, channels), F32),
        pltpu.VMEM((rows, channels), F32),
        pltpu.VMEM((channels, LANES), BF16),
        pltpu.VMEM((plan.filters, LANES), F32),
        pltpu.VMEM((plan.workers * strip, LANES), F32),
        pltpu.VMEM((blocks * strip, LANES), F32),
        pltpu.VMEM((plan.each, rows, blocks * LANES), BF16),
        pltpu.VMEM((blocks * plan.group, LANES), F32),
        pltpu.VMEM((channels, LANES), BF16),
        pltpu.VMEM((plan.halves, rows, LANES), F32),
    ]
    scratch += [pltpu.VMEM(part_piece, BF16)] * parts
    scratch += [pltpu.VMEM((plan.each_part, blocks * plan.group, LANES), BF16)] * parts
    scratch += [pltpu.VMEM(part_piece, BF16)] * parts
    scratch += [pltpu.VMEM(part_piece, BF16)] * parts
    scratch += [sems((1,)), sems((1,)), sems((plan.halves,)), sems((plan.halves,))]
    scratch += [sems((6,)), sems((parts, 2))]
    scratch += [sems((parts,))] * 4
    pairs = blocks * (blocks + 2) // 4
    return pl.pallas_call(
        functools.partial(kernel, plan),
        out_shape=jax.ShapeDtypeStruct((rows, channels), BF16),
        in_specs=[hbm] * 7,
        out_specs=vmem,
        scratch_shapes=scratch,
        compiler_params=pltpu.CompilerParams(
            collective_id=0, has_side_effects=True, vmem_limit_bytes=VMEM_BYTES
        ),
        cost_estimate=pl.CostEstimate(
            flops=2 * plan.each * pairs * plan.group * rows * 2 * LANES,
            bytes_accessed=8 * rows * channels,
            transcendentals=0,
        ),
    )(pair_list.T, query, key, value, filter_taps, conv_bias[None, :], norm_gain[None, :])


def solution(mesh):
    placed = (P("ctx", "ch"), P("ctx", "ch"), P("ctx", "ch"), P("ctx", "ch"), P("ch"), P("ch"), P())
    return jax.shard_map(
        functools.partial(body, mesh),
        mesh=mesh,
        in_specs=placed,
        out_specs=P("ctx", "ch"),
        check_vma=False,
    )
```

```python
import functools

import jax
import jax.numpy as jnp
from jax import lax
from jax.experimental import pallas as pl
from jax.experimental.pallas import tpu as pltpu
from jax.sharding import PartitionSpec as P

MESH = pl.DeviceIdType.MESH
LANES = 128
VMEM_BYTES = 852 * 64 * 1024
STRIP = 8
F32 = jnp.float32
BF16 = jnp.bfloat16


class Plan:
    def __init__(self, mesh, channels, filters, rows):
        self.blocks = mesh.shape["ctx"]
        self.halves = mesh.shape["ch"]
        self.rows = rows
        self.channels = channels
        self.filters = filters
        self.group = channels // filters
        self.each = max(1, filters // self.blocks)
        self.workers = filters // self.each
        self.share = self.each * self.group
        self.parts = 4 if self.each % 4 == 0 else 1
        self.each_part = self.each // self.parts
        self.share_part = self.share // self.parts
        self.span = channels // self.parts


def kernel(plan, pairs, query, key, value, taps, bias, gain, out, *scratch):
    blocks, rows, group, span = plan.blocks, plan.rows, plan.group, plan.span
    part_rows = plan.share_part
    parts = range(plan.parts)
    scratch = list(scratch)
    take = lambda count: [scratch.pop(0) for _ in range(count)]
    pairs_here, table, table_here, query_here, key_here, value_here, taps_here, bias_here = take(8)
    gain_here, gated = take(2)
    flipped, taps_rows, taps_flipped, taps_got, toeplitz, total, results, squares = take(8)
    got, ordered, made, staged = (take(plan.parts) for _ in range(4))
    taps_send, taps_recv, square_send, square_recv, loaded, loaded_part = take(6)
    go_send, go_recv, back_send, back_recv = take(4)

    me = lax.axis_index("ctx")
    half = lax.axis_index("ch")

    def only_worker(index):
        if plan.workers == blocks:
            return lambda fn: fn()
        return pl.when(index < plan.workers)

    def slot_of(step):
        return lax.rem(me + step, blocks)

    bits = [1 << place for place in range((blocks - 1).bit_length())]
    digits = [lax.rem(lax.div(me, bit), 2) for bit in bits]

    def peer_of(mask):
        peer = me
        for bit, digit in zip(bits, digits):
            flip = (mask // bit) % 2 if isinstance(mask, int) else lax.rem(lax.div(mask, bit), 2)
            peer = peer + flip * bit * (1 - 2 * digit)
        return peer

    near = [peer_of(blocks - step) for step in range(1, blocks)] if blocks <= 16 else None

    def each_peer(act):
        if near is not None:
            for peer in near:
                act(peer)
        else:
            pl.loop(1, blocks)(lambda step: act(peer_of(blocks - step)))

    def spread(count, act):
        if count <= 16:
            for index in range(count):
                act(index)
        else:
            pl.loop(0, count)(act)

    def column_copies(part):
        at = pl.ds(part * span, span)
        return [
            pltpu.make_async_copy(there.at[:, at], here.at[:, at], loaded_part.at[part, place])
            for place, (there, here) in enumerate(((key, key_here), (value, value_here)))
        ]

    whole_copies = [
        pltpu.make_async_copy(there, here, loaded.at[place])
        for place, (there, here) in enumerate(
            ((taps, taps_here), (pairs, pairs_here), (bias, bias_here), (query, query_here), (gain, gain_here))
        )
    ]
    taps_load, pairs_load, bias_load, query_load, gain_load = whole_copies
    table_load = pltpu.make_async_copy(table, table_here, loaded.at[5])

    strip = taps_flipped.shape[0] // plan.workers

    def strip_of(index):
        return pl.ds(pl.multiple_of(index * strip, strip), strip)

    def arrived(ref, sem):
        pltpu.make_async_remote_copy(
            src_ref=ref,
            dst_ref=ref,
            send_sem=sem,
            recv_sem=sem,
            device_id={"ctx": slot_of(1)},
            device_id_type=MESH,
        ).wait_recv()

    def from_others(wait):
        if plan.workers == blocks:
            wait(blocks - 1)
        else:
            pl.when(me < plan.workers)(lambda: wait(plan.workers - 1))
            pl.when(me >= plan.workers)(lambda: wait(plan.workers))

    def taps_copy(peer, slot):
        return pltpu.make_async_remote_copy(
            src_ref=taps_flipped.at[strip_of(peer)],
            dst_ref=taps_got.at[strip_of(slot)],
            send_sem=taps_send.at[0],
            recv_sem=taps_recv.at[0],
            device_id={"ctx": peer},
            device_id_type=MESH,
        )

    def go_copy(part, peer, slot):
        first = pl.multiple_of(part * span + peer * part_rows, group)
        return pltpu.make_async_remote_copy(
            src_ref=flipped.at[pl.ds(first, part_rows)],
            dst_ref=got[part].at[slot],
            send_sem=go_send.at[part],
            recv_sem=go_recv.at[part],
            device_id={"ctx": peer},
            device_id_type=MESH,
        )

    def back_copy(part, peer, slot):
        first = pl.multiple_of(part * span + slot * part_rows, group)
        return pltpu.make_async_remote_copy(
            src_ref=staged[part].at[peer],
            dst_ref=results.at[pl.ds(first, part_rows)],
            send_sem=back_send.at[part],
            recv_sem=back_recv.at[part],
            device_id={"ctx": peer},
            device_id_type=MESH,
        )

    def square_copy(peer, slot):
        return pltpu.make_async_remote_copy(
            src_ref=squares.at[half],
            dst_ref=squares.at[slot],
            send_sem=square_send.at[peer],
            recv_sem=square_recv.at[slot],
            device_id={"ch": peer},
            device_id_type=MESH,
        )

    barrier = pltpu.get_barrier_semaphore()

    @each_peer
    def _(peer):
        pl.semaphore_signal(barrier, inc=1, device_id={"ctx": peer}, device_id_type=MESH)

    for step in range(1, plan.halves):
        pl.semaphore_signal(
            barrier,
            inc=1,
            device_id={"ch": lax.rem(half + step, plan.halves)},
            device_id_type=MESH,
        )

    taps_load.start()
    for part in parts:
        for copy in column_copies(part):
            copy.start()
    for copy in (pairs_load, bias_load, query_load, gain_load):
        copy.start()

    taps_load.wait()
    taps_rows[...] = jnp.transpose(taps_here[...])

    for part in parts:
        for index in range(plan.each_part):
            row = part * (plan.filters // plan.parts) + index
            taps_flipped[pl.ds(part * plan.each_part + index, plan.workers, stride=strip), :] = (
                taps_rows[pl.ds(row, plan.workers, stride=plan.each_part), :]
            )

    def signal_tile(columns):
        return key_here[:, columns].astype(F32) * value_here[:, columns].astype(F32)

    part_tiles = span // LANES

    for part in parts:
        for copy in column_copies(part):
            copy.wait()

        for tile in range(part * part_tiles, (part + 1) * part_tiles):
            at = pl.ds(tile * LANES, LANES)
            flipped[at, :] = jnp.transpose(signal_tile(at)).astype(BF16)

        if part == 0:
            pl.semaphore_wait(barrier, blocks - 1 + plan.halves - 1)

            @each_peer
            def _(peer):
                @only_worker(peer)
                def _():
                    taps_copy(peer, me).start()

        @each_peer
        def _(peer, part=part):
            @only_worker(peer)
            def _():
                go_copy(part, peer, me).start()

    pairs_load.wait()
    source, target, runner = (pairs_here[place : place + 1, :] for place in range(3))
    slots = lax.broadcasted_iota(jnp.int32, (blocks, pairs_here.shape[1]), 0)
    diagonal = source == target
    device_of = jnp.where(diagonal & (source == slots), runner, 0)
    holder = jnp.where(diagonal & (runner == slots), source, 0)
    for place, found in enumerate((device_of, holder)):
        table[place * blocks : (place + 1) * blocks, :] = jnp.broadcast_to(
            jnp.sum(found, axis=1, keepdims=True), (blocks, LANES)
        )
    table_load.start()

    ahead = lax.broadcasted_iota(jnp.int32, (rows, LANES), 1) >= lax.broadcasted_iota(
        jnp.int32, (rows, LANES), 0
    )
    run = 8

    def spread_taps(part):
        @pl.loop(part * plan.each_part, (part + 1) * plan.each_part)
        def _(index):
            def some(step, before):
                for block in [step * run + place for place in range(run)]:
                    line = taps_got[pl.ds(block * strip + index, 1), :]
                    turned = pltpu.roll(
                        jnp.broadcast_to(line, (rows, LANES)), 0, 1, stride=1, stride_axis=0
                    )
                    at = pl.ds(pl.multiple_of(block * LANES, LANES), LANES)
                    toeplitz[index, :, at] = jnp.where(ahead, turned, before).astype(BF16)
                    before = turned
                return before

            lax.fori_loop(0, blocks // run, some, jnp.zeros((rows, LANES), F32))

    @only_worker(me)
    def _():
        taps_got[strip_of(me), :] = taps_flipped[strip_of(me), :]
        for part in parts:
            first = pl.multiple_of(part * span + me * part_rows, group)
            got[part][me] = flipped[pl.ds(first, part_rows), :]

        arrived(taps_got.at[pl.ds(0, (blocks - 1) * strip)], taps_recv.at[0])
        spread_taps(0)

    table_load.wait()

    @only_worker(me)
    def _():
        for part in parts:
            if part > 0:
                spread_taps(part)

            arrived(got[part].at[pl.ds(0, blocks - 1)], go_recv.at[part])

            def in_order(block, part=part):
                piece = got[part][table_here[block, 0]]
                at = pl.ds(block * group, group)
                for index in range(plan.each_part):
                    ordered[part][index, at, :] = piece[index * group : (index + 1) * group]

            spread(blocks, in_order)

            @pl.loop(0, plan.each_part)
            def _(index, part=part):
                for pair in range(blocks // 2):
                    height = (blocks - 2 * pair) * group
                    product = jnp.dot(
                        ordered[part][index, :height, :],
                        toeplitz[
                            part * plan.each_part + index,
                            :,
                            2 * pair * LANES : 2 * (pair + 1) * LANES,
                        ],
                        preferred_element_type=F32,
                    )
                    even, odd = 2 * pair * group, (2 * pair + 1) * group
                    if pair == 0:
                        total[...] = product[:, :LANES]
                    else:
                        total[even:, :] += product[:, :LANES]
                    total[odd:, :] += product[: height - group, LANES:]
                at = pl.ds(pl.multiple_of(index * group, group), group)
                made[part][:, at, :] = total[...].astype(BF16).reshape(blocks, group, LANES)

            @each_peer
            def _(peer, part=part):
                staged[part][peer] = made[part][table_here[blocks + peer, 0]]
                back_copy(part, peer, me).start()

            first = pl.multiple_of(part * span + me * part_rows, group)
            results[pl.ds(first, part_rows), :] = made[part][table_here[blocks + me, 0]]

    bias_load.wait()
    query_load.wait()
    sums = jnp.zeros((rows, LANES), F32)
    for part in parts:

        from_others(
            lambda count, part=part: arrived(
                results.at[pl.ds(part * span, count * part_rows)], back_recv.at[part]
            )
        )

        for tile in range(part * part_tiles, (part + 1) * part_tiles):
            at = pl.ds(tile * LANES, LANES)
            conv = jnp.transpose(results[at, :].astype(F32))
            signal = signal_tile(at).astype(BF16).astype(F32)
            product = query_here[:, at].astype(F32) * (conv + bias_here[:, at] * signal)
            gated[:, at] = product
            sums = sums + product * product

    squares[half] = jnp.broadcast_to(jnp.sum(sums, axis=1, keepdims=True), (rows, LANES))
    for step in range(1, plan.halves):
        square_copy(lax.rem(half + step, plan.halves), half).start()

    from_others(
        lambda count: arrived(taps_flipped.at[pl.ds(0, count * strip)], taps_send.at[0])
    )
    for part in parts:
        from_others(
            lambda count, part=part: arrived(
                flipped.at[pl.ds(part * span, count * part_rows)], go_send.at[part]
            )
        )

    @only_worker(me)
    def _():
        for part in parts:
            arrived(staged[part].at[pl.ds(0, blocks - 1)], back_send.at[part])

    for step in range(1, plan.halves):
        square_copy(half, lax.rem(half + step, plan.halves)).wait_recv()
    whole = squares[0]
    for other in range(1, plan.halves):
        whole = whole + squares[other]
    scaling = lax.rsqrt(whole / (plan.channels * plan.halves) + 1e-05)
    gain_load.wait()

    for tile in range(plan.channels // LANES):
        at = pl.ds(tile * LANES, LANES)
        out[:, at] = (gated[:, at] * scaling * gain_here[:, at]).astype(BF16)

    for step in range(1, plan.halves):
        square_copy(lax.rem(half + step, plan.halves), half).wait_send()


def body(mesh, query, key, value, filter_taps, conv_bias, norm_gain, pair_list):
    rows, channels = query.shape
    plan = Plan(mesh, channels, filter_taps.shape[1], rows)
    blocks, parts = plan.blocks, plan.parts
    vmem = pl.BlockSpec(memory_space=pltpu.VMEM)
    hbm = pl.BlockSpec(memory_space=pltpu.HBM)
    strip = max(STRIP, plan.each)
    part_piece = (blocks, plan.share_part, LANES)
    sems = pltpu.SemaphoreType.DMA
    scratch = [
        pltpu.VMEM(pair_list.shape[::-1], jnp.int32),
        pltpu.VMEM((2 * blocks, LANES), jnp.int32),
        pltpu.SMEM((2 * blocks, LANES), jnp.int32),
        pltpu.VMEM((rows, channels), BF16),
        pltpu.VMEM((rows, channels), BF16),
        pltpu.VMEM((rows, channels), BF16),
        pltpu.VMEM(filter_taps.shape, F32),
        pltpu.VMEM((1, channels), F32),
        pltpu.VMEM((1, channels), F32),
        pltpu.VMEM((rows, channels), F32),
        pltpu.VMEM((channels, LANES), BF16),
        pltpu.VMEM((plan.filters, LANES), F32),
        pltpu.VMEM((plan.workers * strip, LANES), F32),
        pltpu.VMEM((blocks * strip, LANES), F32),
        pltpu.VMEM((plan.each, rows, blocks * LANES), BF16),
        pltpu.VMEM((blocks * plan.group, LANES), F32),
        pltpu.VMEM((channels, LANES), BF16),
        pltpu.VMEM((plan.halves, rows, LANES), F32),
    ]
    scratch += [pltpu.VMEM(part_piece, BF16)] * parts
    scratch += [pltpu.VMEM((plan.each_part, blocks * plan.group, LANES), BF16)] * parts
    scratch += [pltpu.VMEM(part_piece, BF16)] * parts
    scratch += [pltpu.VMEM(part_piece, BF16)] * parts
    scratch += [sems((1,)), sems((1,)), sems((plan.halves,)), sems((plan.halves,))]
    scratch += [sems((6,)), sems((parts, 2))]
    scratch += [sems((parts,))] * 4
    pairs = blocks * (blocks + 2) // 4
    return pl.pallas_call(
        functools.partial(kernel, plan),
        out_shape=jax.ShapeDtypeStruct((rows, channels), BF16),
        in_specs=[hbm] * 7,
        out_specs=vmem,
        scratch_shapes=scratch,
        compiler_params=pltpu.CompilerParams(
            collective_id=0, has_side_effects=True, vmem_limit_bytes=VMEM_BYTES
        ),
        cost_estimate=pl.CostEstimate(
            flops=2 * plan.each * pairs * plan.group * rows * 2 * LANES,
            bytes_accessed=8 * rows * channels,
            transcendentals=0,
        ),
    )(pair_list.T, query, key, value, filter_taps, conv_bias[None, :], norm_gain[None, :])


def solution(mesh):
    placed = (P("ctx", "ch"), P("ctx", "ch"), P("ctx", "ch"), P("ctx", "ch"), P("ch"), P("ch"), P())
    return jax.shard_map(
        functools.partial(body, mesh),
        mesh=mesh,
        in_specs=placed,
        out_specs=P("ctx", "ch"),
        check_vma=False,
    )
```

```python
import functools

import jax
import jax.numpy as jnp
from jax import lax
from jax.experimental import pallas as pl
from jax.experimental.pallas import tpu as pltpu
from jax.sharding import PartitionSpec as P

MESH = pl.DeviceIdType.MESH
LANES = 128
VMEM_BYTES = 1013 * 64 * 1024
STRIP = 8
F32 = jnp.float32
BF16 = jnp.bfloat16


class Plan:
    def __init__(self, mesh, channels, filters, rows):
        self.blocks = mesh.shape["ctx"]
        self.halves = mesh.shape["ch"]
        self.rows = rows
        self.channels = channels
        self.filters = filters
        self.group = channels // filters
        self.each = max(1, filters // self.blocks)
        self.workers = filters // self.each
        self.share = self.each * self.group
        self.parts = 4 if self.each % 4 == 0 else 1
        self.each_part = self.each // self.parts
        self.share_part = self.share // self.parts
        self.span = channels // self.parts


def kernel(plan, pairs, query, key, value, taps, bias, gated_out, scale, *scratch):
    blocks, rows, group, span = plan.blocks, plan.rows, plan.group, plan.span
    part_rows = plan.share_part
    parts = range(plan.parts)
    scratch = list(scratch)
    take = lambda count: [scratch.pop(0) for _ in range(count)]
    pairs_here, table, table_here, query_here, key_here, value_here, taps_here, bias_here = take(8)
    (gated,) = take(1)
    flipped, taps_rows, taps_flipped, taps_got, toeplitz, total, results, squares = take(8)
    got, ordered, made, staged = (take(plan.parts) for _ in range(4))
    taps_send, taps_recv, square_send, square_recv, loaded, loaded_part, stored = take(7)
    go_send, go_recv, back_send, back_recv = take(4)

    me = lax.axis_index("ctx")
    half = lax.axis_index("ch")

    def only_worker(index):
        if plan.workers == blocks:
            return lambda fn: fn()
        return pl.when(index < plan.workers)

    def slot_of(step):
        return lax.rem(me + step, blocks)

    bits = [1 << place for place in range((blocks - 1).bit_length())]
    digits = [lax.rem(lax.div(me, bit), 2) for bit in bits]

    def peer_of(mask):
        peer = me
        for bit, digit in zip(bits, digits):
            flip = (mask // bit) % 2 if isinstance(mask, int) else lax.rem(lax.div(mask, bit), 2)
            peer = peer + flip * bit * (1 - 2 * digit)
        return peer

    near = [peer_of(blocks - step) for step in range(1, blocks)] if blocks <= 16 else None

    def each_peer(act):
        if near is not None:
            for peer in near:
                act(peer)
        else:
            pl.loop(1, blocks)(lambda step: act(peer_of(blocks - step)))

    def spread(count, act):
        if count <= 16:
            for index in range(count):
                act(index)
        else:
            pl.loop(0, count)(act)

    def column_copies(part):
        at = pl.ds(part * span, span)
        return [
            pltpu.make_async_copy(there.at[:, at], here.at[:, at], loaded_part.at[part, place])
            for place, (there, here) in enumerate(((key, key_here), (value, value_here)))
        ]

    def gated_store(part):
        at = pl.ds(part * span, span)
        return pltpu.make_async_copy(gated.at[:, at], gated_out.at[:, at], stored.at[part])

    whole_copies = [
        pltpu.make_async_copy(there, here, loaded.at[place])
        for place, (there, here) in enumerate(
            ((taps, taps_here), (pairs, pairs_here), (bias, bias_here), (query, query_here))
        )
    ]
    taps_load, pairs_load, bias_load, query_load = whole_copies
    table_load = pltpu.make_async_copy(table, table_here, loaded.at[4])

    strip = taps_flipped.shape[0] // plan.workers

    def strip_of(index):
        return pl.ds(pl.multiple_of(index * strip, strip), strip)

    def arrived(ref, sem):
        pltpu.make_async_remote_copy(
            src_ref=ref,
            dst_ref=ref,
            send_sem=sem,
            recv_sem=sem,
            device_id={"ctx": slot_of(1)},
            device_id_type=MESH,
        ).wait_recv()

    def from_others(wait):
        if plan.workers == blocks:
            wait(blocks - 1)
        else:
            pl.when(me < plan.workers)(lambda: wait(plan.workers - 1))
            pl.when(me >= plan.workers)(lambda: wait(plan.workers))

    def taps_copy(peer, slot):
        return pltpu.make_async_remote_copy(
            src_ref=taps_flipped.at[strip_of(peer)],
            dst_ref=taps_got.at[strip_of(slot)],
            send_sem=taps_send.at[0],
            recv_sem=taps_recv.at[0],
            device_id={"ctx": peer},
            device_id_type=MESH,
        )

    def go_copy(part, peer, slot):
        first = pl.multiple_of(part * span + peer * part_rows, group)
        return pltpu.make_async_remote_copy(
            src_ref=flipped.at[pl.ds(first, part_rows)],
            dst_ref=got[part].at[slot],
            send_sem=go_send.at[part],
            recv_sem=go_recv.at[part],
            device_id={"ctx": peer},
            device_id_type=MESH,
        )

    def back_copy(part, peer, slot):
        first = pl.multiple_of(part * span + slot * part_rows, group)
        return pltpu.make_async_remote_copy(
            src_ref=staged[part].at[peer],
            dst_ref=results.at[pl.ds(first, part_rows)],
            send_sem=back_send.at[part],
            recv_sem=back_recv.at[part],
            device_id={"ctx": peer},
            device_id_type=MESH,
        )

    def square_copy(peer, slot):
        return pltpu.make_async_remote_copy(
            src_ref=squares.at[half],
            dst_ref=squares.at[slot],
            send_sem=square_send.at[peer],
            recv_sem=square_recv.at[slot],
            device_id={"ch": peer},
            device_id_type=MESH,
        )

    barrier = pltpu.get_barrier_semaphore()

    @each_peer
    def _(peer):
        pl.semaphore_signal(barrier, inc=1, device_id={"ctx": peer}, device_id_type=MESH)

    for step in range(1, plan.halves):
        pl.semaphore_signal(
            barrier,
            inc=1,
            device_id={"ch": lax.rem(half + step, plan.halves)},
            device_id_type=MESH,
        )

    taps_load.start()
    for part in parts:
        for copy in column_copies(part):
            copy.start()
    for copy in (pairs_load, bias_load, query_load):
        copy.start()

    taps_load.wait()
    taps_rows[...] = jnp.transpose(taps_here[...])

    for part in parts:
        for index in range(plan.each_part):
            row = part * (plan.filters // plan.parts) + index
            taps_flipped[pl.ds(part * plan.each_part + index, plan.workers, stride=strip), :] = (
                taps_rows[pl.ds(row, plan.workers, stride=plan.each_part), :]
            )

    def signal_tile(columns):
        return key_here[:, columns].astype(F32) * value_here[:, columns].astype(F32)

    part_tiles = span // LANES

    for part in parts:
        for copy in column_copies(part):
            copy.wait()

        for tile in range(part * part_tiles, (part + 1) * part_tiles):
            at = pl.ds(tile * LANES, LANES)
            flipped[at, :] = jnp.transpose(signal_tile(at)).astype(BF16)

        if part == 0:
            pl.semaphore_wait(barrier, blocks - 1 + plan.halves - 1)

            @each_peer
            def _(peer):
                @only_worker(peer)
                def _():
                    taps_copy(peer, me).start()

        @each_peer
        def _(peer, part=part):
            @only_worker(peer)
            def _():
                go_copy(part, peer, me).start()

    pairs_load.wait()
    source, target, runner = (pairs_here[place : place + 1, :] for place in range(3))
    slots = lax.broadcasted_iota(jnp.int32, (blocks, pairs_here.shape[1]), 0)
    diagonal = source == target
    device_of = jnp.where(diagonal & (source == slots), runner, 0)
    holder = jnp.where(diagonal & (runner == slots), source, 0)
    for place, found in enumerate((device_of, holder)):
        table[place * blocks : (place + 1) * blocks, :] = jnp.broadcast_to(
            jnp.sum(found, axis=1, keepdims=True), (blocks, LANES)
        )
    table_load.start()

    ahead = lax.broadcasted_iota(jnp.int32, (rows, LANES), 1) >= lax.broadcasted_iota(
        jnp.int32, (rows, LANES), 0
    )
    run = 8

    def spread_taps(part):
        @pl.loop(part * plan.each_part, (part + 1) * plan.each_part)
        def _(index):
            def some(step, before):
                for block in [step * run + place for place in range(run)]:
                    line = taps_got[pl.ds(block * strip + index, 1), :]
                    turned = pltpu.roll(
                        jnp.broadcast_to(line, (rows, LANES)), 0, 1, stride=1, stride_axis=0
                    )
                    at = pl.ds(pl.multiple_of(block * LANES, LANES), LANES)
                    toeplitz[index, :, at] = jnp.where(ahead, turned, before).astype(BF16)
                    before = turned
                return before

            lax.fori_loop(0, blocks // run, some, jnp.zeros((rows, LANES), F32))

    @only_worker(me)
    def _():
        taps_got[strip_of(me), :] = taps_flipped[strip_of(me), :]
        for part in parts:
            first = pl.multiple_of(part * span + me * part_rows, group)
            got[part][me] = flipped[pl.ds(first, part_rows), :]

        arrived(taps_got.at[pl.ds(0, (blocks - 1) * strip)], taps_recv.at[0])
        spread_taps(0)

    table_load.wait()

    @only_worker(me)
    def _():
        for part in parts:
            if part > 0:
                spread_taps(part)

            arrived(got[part].at[pl.ds(0, blocks - 1)], go_recv.at[part])

            def in_order(block, part=part):
                piece = got[part][table_here[block, 0]]
                at = pl.ds(block * group, group)
                for index in range(plan.each_part):
                    ordered[part][index, at, :] = piece[index * group : (index + 1) * group]

            spread(blocks, in_order)

            @pl.loop(0, plan.each_part)
            def _(index, part=part):
                for pair in range(blocks // 2):
                    height = (blocks - 2 * pair) * group
                    product = jnp.dot(
                        ordered[part][index, :height, :],
                        toeplitz[
                            part * plan.each_part + index,
                            :,
                            2 * pair * LANES : 2 * (pair + 1) * LANES,
                        ],
                        preferred_element_type=F32,
                    )
                    even, odd = 2 * pair * group, (2 * pair + 1) * group
                    if pair == 0:
                        total[...] = product[:, :LANES]
                    else:
                        total[even:, :] += product[:, :LANES]
                    total[odd:, :] += product[: height - group, LANES:]
                at = pl.ds(pl.multiple_of(index * group, group), group)
                made[part][:, at, :] = total[...].astype(BF16).reshape(blocks, group, LANES)

            @each_peer
            def _(peer, part=part):
                staged[part][peer] = made[part][table_here[blocks + peer, 0]]
                back_copy(part, peer, me).start()

            first = pl.multiple_of(part * span + me * part_rows, group)
            results[pl.ds(first, part_rows), :] = made[part][table_here[blocks + me, 0]]

    bias_load.wait()
    query_load.wait()
    sums = jnp.zeros((rows, LANES), F32)
    for part in parts:

        from_others(
            lambda count, part=part: arrived(
                results.at[pl.ds(part * span, count * part_rows)], back_recv.at[part]
            )
        )

        for tile in range(part * part_tiles, (part + 1) * part_tiles):
            at = pl.ds(tile * LANES, LANES)
            conv = jnp.transpose(results[at, :].astype(F32))
            signal = signal_tile(at).astype(BF16).astype(F32)
            product = query_here[:, at].astype(F32) * (conv + bias_here[:, at] * signal)
            gated[:, at] = product
            sums = sums + product * product
        gated_store(part).start()

    squares[half] = jnp.broadcast_to(jnp.sum(sums, axis=1, keepdims=True), (rows, LANES))
    for step in range(1, plan.halves):
        square_copy(lax.rem(half + step, plan.halves), half).start()

    from_others(
        lambda count: arrived(taps_flipped.at[pl.ds(0, count * strip)], taps_send.at[0])
    )
    for part in parts:
        from_others(
            lambda count, part=part: arrived(
                flipped.at[pl.ds(part * span, count * part_rows)], go_send.at[part]
            )
        )

    @only_worker(me)
    def _():
        for part in parts:
            arrived(staged[part].at[pl.ds(0, blocks - 1)], back_send.at[part])

    for step in range(1, plan.halves):
        square_copy(half, lax.rem(half + step, plan.halves)).wait_recv()
    whole = squares[0]
    for other in range(1, plan.halves):
        whole = whole + squares[other]
    scale[...] = lax.rsqrt(whole / (plan.channels * plan.halves) + 1e-05)
    for part in parts:
        gated_store(part).wait()
    for step in range(1, plan.halves):
        square_copy(lax.rem(half + step, plan.halves), half).wait_send()


def rescale(pieces, gated, scale, gain, out, *scratch):
    gated_here, scale_here, gain_here, out_here, small, loaded, stored = scratch
    width = gated.shape[1] // pieces
    columns = [pl.ds(piece * width, width) for piece in range(pieces)]
    loads = [
        pltpu.make_async_copy(gated.at[:, at], gated_here.at[:, at], loaded.at[piece])
        for piece, at in enumerate(columns)
    ]
    stores = [
        pltpu.make_async_copy(out_here.at[:, at], out.at[:, at], stored.at[piece])
        for piece, at in enumerate(columns)
    ]
    scale_load = pltpu.make_async_copy(scale, scale_here, small.at[0])
    gain_load = pltpu.make_async_copy(gain, gain_here, small.at[1])
    for copy in [scale_load, gain_load] + loads:
        copy.start()
    scale_load.wait()
    gain_load.wait()
    for piece in range(pieces):
        loads[piece].wait()
        for first in range(piece * width, (piece + 1) * width, LANES):
            at = pl.ds(first, LANES)
            out_here[:, at] = (gated_here[:, at] * scale_here[...] * gain_here[:, at]).astype(BF16)
        stores[piece].start()
    for store in stores:
        store.wait()


def body(mesh, query, key, value, filter_taps, conv_bias, norm_gain, pair_list):
    rows, channels = query.shape
    plan = Plan(mesh, channels, filter_taps.shape[1], rows)
    blocks, parts = plan.blocks, plan.parts
    vmem = pl.BlockSpec(memory_space=pltpu.VMEM)
    hbm = pl.BlockSpec(memory_space=pltpu.HBM)
    strip = max(STRIP, plan.each)
    part_piece = (blocks, plan.share_part, LANES)
    sems = pltpu.SemaphoreType.DMA
    scratch = [
        pltpu.VMEM(pair_list.shape[::-1], jnp.int32),
        pltpu.VMEM((2 * blocks, LANES), jnp.int32),
        pltpu.SMEM((2 * blocks, LANES), jnp.int32),
        pltpu.VMEM((rows, channels), BF16),
        pltpu.VMEM((rows, channels), BF16),
        pltpu.VMEM((rows, channels), BF16),
        pltpu.VMEM(filter_taps.shape, F32),
        pltpu.VMEM((1, channels), F32),
        pltpu.VMEM((rows, channels), F32),
        pltpu.VMEM((channels, LANES), BF16),
        pltpu.VMEM((plan.filters, LANES), F32),
        pltpu.VMEM((plan.workers * strip, LANES), F32),
        pltpu.VMEM((blocks * strip, LANES), F32),
        pltpu.VMEM((plan.each, rows, blocks * LANES), BF16),
        pltpu.VMEM((blocks * plan.group, LANES), F32),
        pltpu.VMEM((channels, LANES), BF16),
        pltpu.VMEM((plan.halves, rows, LANES), F32),
    ]
    scratch += [pltpu.VMEM(part_piece, BF16)] * parts
    scratch += [pltpu.VMEM((plan.each_part, blocks * plan.group, LANES), BF16)] * parts
    scratch += [pltpu.VMEM(part_piece, BF16)] * parts
    scratch += [pltpu.VMEM(part_piece, BF16)] * parts
    scratch += [sems((1,)), sems((1,)), sems((plan.halves,)), sems((plan.halves,))]
    scratch += [sems((5,)), sems((parts, 2)), sems((parts,))]
    scratch += [sems((parts,))] * 4
    pairs = blocks * (blocks + 2) // 4
    gated, scale = pl.pallas_call(
        functools.partial(kernel, plan),
        out_shape=(
            jax.ShapeDtypeStruct((rows, channels), F32),
            jax.ShapeDtypeStruct((rows, LANES), F32),
        ),
        in_specs=[hbm] * 6,
        out_specs=(hbm, vmem),
        scratch_shapes=scratch,
        compiler_params=pltpu.CompilerParams(
            collective_id=0, has_side_effects=True, vmem_limit_bytes=VMEM_BYTES
        ),
        cost_estimate=pl.CostEstimate(
            flops=2 * plan.each * pairs * plan.group * rows * 2 * LANES,
            bytes_accessed=8 * rows * channels,
            transcendentals=0,
        ),
    )(pair_list.T, query, key, value, filter_taps, conv_bias[None, :])
    pieces = 4
    return pl.pallas_call(
        functools.partial(rescale, pieces),
        out_shape=jax.ShapeDtypeStruct((rows, channels), BF16),
        in_specs=[hbm] * 3,
        out_specs=hbm,
        scratch_shapes=[
            pltpu.VMEM((rows, channels), F32),
            pltpu.VMEM((rows, LANES), F32),
            pltpu.VMEM((1, channels), F32),
            pltpu.VMEM((rows, channels), BF16),
            sems((2,)),
            sems((pieces,)),
            sems((pieces,)),
        ],
        compiler_params=pltpu.CompilerParams(vmem_limit_bytes=VMEM_BYTES),
        cost_estimate=pl.CostEstimate(
            flops=2 * rows * channels, bytes_accessed=6 * rows * channels, transcendentals=0
        ),
    )(gated, scale, norm_gain[None, :])


def solution(mesh):
    placed = (P("ctx", "ch"), P("ctx", "ch"), P("ctx", "ch"), P("ctx", "ch"), P("ch"), P("ch"), P())
    return jax.shard_map(
        functools.partial(body, mesh),
        mesh=mesh,
        in_specs=placed,
        out_specs=P("ctx", "ch"),
        check_vma=False,
    )
```

```python
import functools

import jax
import jax.numpy as jnp
from jax import lax
from jax.experimental import pallas as pl
from jax.experimental.pallas import tpu as pltpu
from jax.sharding import PartitionSpec as P

MESH = pl.DeviceIdType.MESH
LANES = 128
VMEM_BYTES = 1013 * 64 * 1024
STRIP = 8
F32 = jnp.float32
BF16 = jnp.bfloat16


class Plan:
    def __init__(self, mesh, channels, filters, rows):
        self.blocks = mesh.shape["ctx"]
        self.halves = mesh.shape["ch"]
        self.rows = rows
        self.channels = channels
        self.filters = filters
        self.group = channels // filters
        self.each = max(1, filters // self.blocks)
        self.workers = filters // self.each
        self.share = self.each * self.group
        self.parts = 2 if self.each % 2 == 0 else 1
        self.each_part = self.each // self.parts
        self.share_part = self.share // self.parts
        self.span = channels // self.parts


def kernel(plan, pairs, query, key, value, taps, bias, gated_out, scale, *scratch):
    blocks, rows, group, span = plan.blocks, plan.rows, plan.group, plan.span
    part_rows = plan.share_part
    parts = range(plan.parts)
    scratch = list(scratch)
    take = lambda count: [scratch.pop(0) for _ in range(count)]
    pairs_here, table, table_here, query_here, key_here, value_here, taps_here, bias_here = take(8)
    (gated,) = take(1)
    flipped, taps_rows, taps_flipped, taps_got, toeplitz, total, results, squares = take(8)
    got, ordered, made, staged = (take(plan.parts) for _ in range(4))
    taps_send, taps_recv, square_send, square_recv, loaded, loaded_part, stored = take(7)
    go_send, go_recv, back_send, back_recv = take(4)

    me = lax.axis_index("ctx")
    half = lax.axis_index("ch")

    def only_worker(index):
        if plan.workers == blocks:
            return lambda fn: fn()
        return pl.when(index < plan.workers)

    def slot_of(step):
        return lax.rem(me + step, blocks)

    bits = [1 << place for place in range((blocks - 1).bit_length())]
    digits = [lax.rem(lax.div(me, bit), 2) for bit in bits]

    def peer_of(mask):
        peer = me
        for bit, digit in zip(bits, digits):
            flip = (mask // bit) % 2 if isinstance(mask, int) else lax.rem(lax.div(mask, bit), 2)
            peer = peer + flip * bit * (1 - 2 * digit)
        return peer

    near = [peer_of(blocks - step) for step in range(1, blocks)] if blocks <= 16 else None

    def each_peer(act):
        if near is not None:
            for peer in near:
                act(peer)
        else:
            pl.loop(1, blocks)(lambda step: act(peer_of(blocks - step)))

    def spread(count, act):
        if count <= 16:
            for index in range(count):
                act(index)
        else:
            pl.loop(0, count)(act)

    def column_copies(part):
        at = pl.ds(part * span, span)
        return [
            pltpu.make_async_copy(there.at[:, at], here.at[:, at], loaded_part.at[part, place])
            for place, (there, here) in enumerate(((key, key_here), (value, value_here)))
        ]

    def gated_store(part):
        at = pl.ds(part * span, span)
        return pltpu.make_async_copy(gated.at[:, at], gated_out.at[:, at], stored.at[part])

    whole_copies = [
        pltpu.make_async_copy(there, here, loaded.at[place])
        for place, (there, here) in enumerate(
            ((taps, taps_here), (pairs, pairs_here), (bias, bias_here), (query, query_here))
        )
    ]
    taps_load, pairs_load, bias_load, query_load = whole_copies
    table_load = pltpu.make_async_copy(table, table_here, loaded.at[4])

    strip = taps_flipped.shape[0] // plan.workers

    def strip_of(index):
        return pl.ds(pl.multiple_of(index * strip, strip), strip)

    def arrived(ref, sem):
        pltpu.make_async_remote_copy(
            src_ref=ref,
            dst_ref=ref,
            send_sem=sem,
            recv_sem=sem,
            device_id={"ctx": slot_of(1)},
            device_id_type=MESH,
        ).wait_recv()

    def from_others(wait):
        if plan.workers == blocks:
            wait(blocks - 1)
        else:
            pl.when(me < plan.workers)(lambda: wait(plan.workers - 1))
            pl.when(me >= plan.workers)(lambda: wait(plan.workers))

    def taps_copy(peer, slot):
        return pltpu.make_async_remote_copy(
            src_ref=taps_flipped.at[strip_of(peer)],
            dst_ref=taps_got.at[strip_of(slot)],
            send_sem=taps_send.at[0],
            recv_sem=taps_recv.at[0],
            device_id={"ctx": peer},
            device_id_type=MESH,
        )

    def go_copy(part, peer, slot):
        first = pl.multiple_of(part * span + peer * part_rows, group)
        return pltpu.make_async_remote_copy(
            src_ref=flipped.at[pl.ds(first, part_rows)],
            dst_ref=got[part].at[slot],
            send_sem=go_send.at[part],
            recv_sem=go_recv.at[part],
            device_id={"ctx": peer},
            device_id_type=MESH,
        )

    def back_copy(part, peer, slot):
        first = pl.multiple_of(part * span + slot * part_rows, group)
        return pltpu.make_async_remote_copy(
            src_ref=staged[part].at[peer],
            dst_ref=results.at[pl.ds(first, part_rows)],
            send_sem=back_send.at[part],
            recv_sem=back_recv.at[part],
            device_id={"ctx": peer},
            device_id_type=MESH,
        )

    def square_copy(peer, slot):
        return pltpu.make_async_remote_copy(
            src_ref=squares.at[half],
            dst_ref=squares.at[slot],
            send_sem=square_send.at[peer],
            recv_sem=square_recv.at[slot],
            device_id={"ch": peer},
            device_id_type=MESH,
        )

    barrier = pltpu.get_barrier_semaphore()

    @each_peer
    def _(peer):
        pl.semaphore_signal(barrier, inc=1, device_id={"ctx": peer}, device_id_type=MESH)

    for step in range(1, plan.halves):
        pl.semaphore_signal(
            barrier,
            inc=1,
            device_id={"ch": lax.rem(half + step, plan.halves)},
            device_id_type=MESH,
        )

    taps_load.start()
    for part in parts:
        for copy in column_copies(part):
            copy.start()
    for copy in (pairs_load, bias_load, query_load):
        copy.start()

    taps_load.wait()
    taps_rows[...] = jnp.transpose(taps_here[...])

    for part in parts:
        for index in range(plan.each_part):
            row = part * (plan.filters // plan.parts) + index
            taps_flipped[pl.ds(part * plan.each_part + index, plan.workers, stride=strip), :] = (
                taps_rows[pl.ds(row, plan.workers, stride=plan.each_part), :]
            )

    def signal_tile(columns):
        return key_here[:, columns].astype(F32) * value_here[:, columns].astype(F32)

    part_tiles = span // LANES

    for part in parts:
        for copy in column_copies(part):
            copy.wait()

        for tile in range(part * part_tiles, (part + 1) * part_tiles):
            at = pl.ds(tile * LANES, LANES)
            flipped[at, :] = jnp.transpose(signal_tile(at)).astype(BF16)

        if part == 0:
            pl.semaphore_wait(barrier, blocks - 1 + plan.halves - 1)

            @each_peer
            def _(peer):
                @only_worker(peer)
                def _():
                    taps_copy(peer, me).start()

        @each_peer
        def _(peer, part=part):
            @only_worker(peer)
            def _():
                go_copy(part, peer, me).start()

    pairs_load.wait()
    source, target, runner = (pairs_here[place : place + 1, :] for place in range(3))
    slots = lax.broadcasted_iota(jnp.int32, (blocks, pairs_here.shape[1]), 0)
    diagonal = source == target
    device_of = jnp.where(diagonal & (source == slots), runner, 0)
    holder = jnp.where(diagonal & (runner == slots), source, 0)
    for place, found in enumerate((device_of, holder)):
        table[place * blocks : (place + 1) * blocks, :] = jnp.broadcast_to(
            jnp.sum(found, axis=1, keepdims=True), (blocks, LANES)
        )
    table_load.start()

    ahead = lax.broadcasted_iota(jnp.int32, (rows, LANES), 1) >= lax.broadcasted_iota(
        jnp.int32, (rows, LANES), 0
    )
    run = 8

    def spread_taps(part):
        @pl.loop(part * plan.each_part, (part + 1) * plan.each_part)
        def _(index):
            def some(step, before):
                for block in [step * run + place for place in range(run)]:
                    line = taps_got[pl.ds(block * strip + index, 1), :]
                    turned = pltpu.roll(
                        jnp.broadcast_to(line, (rows, LANES)), 0, 1, stride=1, stride_axis=0
                    )
                    at = pl.ds(pl.multiple_of(block * LANES, LANES), LANES)
                    toeplitz[index, :, at] = jnp.where(ahead, turned, before).astype(BF16)
                    before = turned
                return before

            lax.fori_loop(0, blocks // run, some, jnp.zeros((rows, LANES), F32))

    @only_worker(me)
    def _():
        taps_got[strip_of(me), :] = taps_flipped[strip_of(me), :]
        for part in parts:
            first = pl.multiple_of(part * span + me * part_rows, group)
            got[part][me] = flipped[pl.ds(first, part_rows), :]

        arrived(taps_got.at[pl.ds(0, (blocks - 1) * strip)], taps_recv.at[0])
        spread_taps(0)

    table_load.wait()

    @only_worker(me)
    def _():
        for part in parts:
            if part > 0:
                spread_taps(part)

            arrived(got[part].at[pl.ds(0, blocks - 1)], go_recv.at[part])

            def in_order(block, part=part):
                piece = got[part][table_here[block, 0]]
                at = pl.ds(block * group, group)
                for index in range(plan.each_part):
                    ordered[part][index, at, :] = piece[index * group : (index + 1) * group]

            spread(blocks, in_order)

            @pl.loop(0, plan.each_part)
            def _(index, part=part):
                for pair in range(blocks // 2):
                    height = (blocks - 2 * pair) * group
                    product = jnp.dot(
                        ordered[part][index, :height, :],
                        toeplitz[
                            part * plan.each_part + index,
                            :,
                            2 * pair * LANES : 2 * (pair + 1) * LANES,
                        ],
                        preferred_element_type=F32,
                    )
                    even, odd = 2 * pair * group, (2 * pair + 1) * group
                    if pair == 0:
                        total[...] = product[:, :LANES]
                    else:
                        total[even:, :] += product[:, :LANES]
                    total[odd:, :] += product[: height - group, LANES:]
                at = pl.ds(pl.multiple_of(index * group, group), group)
                made[part][:, at, :] = total[...].astype(BF16).reshape(blocks, group, LANES)

            @each_peer
            def _(peer, part=part):
                staged[part][peer] = made[part][table_here[blocks + peer, 0]]
                back_copy(part, peer, me).start()

            first = pl.multiple_of(part * span + me * part_rows, group)
            results[pl.ds(first, part_rows), :] = made[part][table_here[blocks + me, 0]]

    bias_load.wait()
    query_load.wait()
    sums = jnp.zeros((rows, LANES), F32)
    for part in parts:

        from_others(
            lambda count, part=part: arrived(
                results.at[pl.ds(part * span, count * part_rows)], back_recv.at[part]
            )
        )

        for tile in range(part * part_tiles, (part + 1) * part_tiles):
            at = pl.ds(tile * LANES, LANES)
            conv = jnp.transpose(results[at, :].astype(F32))
            signal = signal_tile(at).astype(BF16).astype(F32)
            product = query_here[:, at].astype(F32) * (conv + bias_here[:, at] * signal)
            gated[:, at] = product
            sums = sums + product * product
        gated_store(part).start()

    squares[half] = jnp.broadcast_to(jnp.sum(sums, axis=1, keepdims=True), (rows, LANES))
    for step in range(1, plan.halves):
        square_copy(lax.rem(half + step, plan.halves), half).start()

    from_others(
        lambda count: arrived(taps_flipped.at[pl.ds(0, count * strip)], taps_send.at[0])
    )
    for part in parts:
        from_others(
            lambda count, part=part: arrived(
                flipped.at[pl.ds(part * span, count * part_rows)], go_send.at[part]
            )
        )

    @only_worker(me)
    def _():
        for part in parts:
            arrived(staged[part].at[pl.ds(0, blocks - 1)], back_send.at[part])

    for step in range(1, plan.halves):
        square_copy(half, lax.rem(half + step, plan.halves)).wait_recv()
    whole = squares[0]
    for other in range(1, plan.halves):
        whole = whole + squares[other]
    scale[...] = lax.rsqrt(whole / (plan.channels * plan.halves) + 1e-05)
    for part in parts:
        gated_store(part).wait()
    for step in range(1, plan.halves):
        square_copy(lax.rem(half + step, plan.halves), half).wait_send()


def rescale(pieces, gated, scale, gain, out, *scratch):
    gated_here, scale_here, gain_here, out_here, small, loaded, stored = scratch
    width = gated.shape[1] // pieces
    columns = [pl.ds(piece * width, width) for piece in range(pieces)]
    loads = [
        pltpu.make_async_copy(gated.at[:, at], gated_here.at[:, at], loaded.at[piece])
        for piece, at in enumerate(columns)
    ]
    stores = [
        pltpu.make_async_copy(out_here.at[:, at], out.at[:, at], stored.at[piece])
        for piece, at in enumerate(columns)
    ]
    scale_load = pltpu.make_async_copy(scale, scale_here, small.at[0])
    gain_load = pltpu.make_async_copy(gain, gain_here, small.at[1])
    for copy in [scale_load, gain_load] + loads:
        copy.start()
    scale_load.wait()
    gain_load.wait()
    for piece in range(pieces):
        loads[piece].wait()
        for first in range(piece * width, (piece + 1) * width, LANES):
            at = pl.ds(first, LANES)
            out_here[:, at] = (gated_here[:, at] * scale_here[...] * gain_here[:, at]).astype(BF16)
        stores[piece].start()
    for store in stores:
        store.wait()


def body(mesh, query, key, value, filter_taps, conv_bias, norm_gain, pair_list):
    rows, channels = query.shape
    plan = Plan(mesh, channels, filter_taps.shape[1], rows)
    blocks, parts = plan.blocks, plan.parts
    vmem = pl.BlockSpec(memory_space=pltpu.VMEM)
    hbm = pl.BlockSpec(memory_space=pltpu.HBM)
    strip = max(STRIP, plan.each)
    part_piece = (blocks, plan.share_part, LANES)
    sems = pltpu.SemaphoreType.DMA
    scratch = [
        pltpu.VMEM(pair_list.shape[::-1], jnp.int32),
        pltpu.VMEM((2 * blocks, LANES), jnp.int32),
        pltpu.SMEM((2 * blocks, LANES), jnp.int32),
        pltpu.VMEM((rows, channels), BF16),
        pltpu.VMEM((rows, channels), BF16),
        pltpu.VMEM((rows, channels), BF16),
        pltpu.VMEM(filter_taps.shape, F32),
        pltpu.VMEM((1, channels), F32),
        pltpu.VMEM((rows, channels), F32),
        pltpu.VMEM((channels, LANES), BF16),
        pltpu.VMEM((plan.filters, LANES), F32),
        pltpu.VMEM((plan.workers * strip, LANES), F32),
        pltpu.VMEM((blocks * strip, LANES), F32),
        pltpu.VMEM((plan.each, rows, blocks * LANES), BF16),
        pltpu.VMEM((blocks * plan.group, LANES), F32),
        pltpu.VMEM((channels, LANES), BF16),
        pltpu.VMEM((plan.halves, rows, LANES), F32),
    ]
    scratch += [pltpu.VMEM(part_piece, BF16)] * parts
    scratch += [pltpu.VMEM((plan.each_part, blocks * plan.group, LANES), BF16)] * parts
    scratch += [pltpu.VMEM(part_piece, BF16)] * parts
    scratch += [pltpu.VMEM(part_piece, BF16)] * parts
    scratch += [sems((1,)), sems((1,)), sems((plan.halves,)), sems((plan.halves,))]
    scratch += [sems((5,)), sems((parts, 2)), sems((parts,))]
    scratch += [sems((parts,))] * 4
    pairs = blocks * (blocks + 2) // 4
    gated, scale = pl.pallas_call(
        functools.partial(kernel, plan),
        out_shape=(
            jax.ShapeDtypeStruct((rows, channels), F32),
            jax.ShapeDtypeStruct((rows, LANES), F32),
        ),
        in_specs=[hbm] * 6,
        out_specs=(hbm, vmem),
        scratch_shapes=scratch,
        compiler_params=pltpu.CompilerParams(
            collective_id=0, has_side_effects=True, vmem_limit_bytes=VMEM_BYTES
        ),
        cost_estimate=pl.CostEstimate(
            flops=2 * plan.each * pairs * plan.group * rows * 2 * LANES,
            bytes_accessed=8 * rows * channels,
            transcendentals=0,
        ),
    )(pair_list.T, query, key, value, filter_taps, conv_bias[None, :])
    pieces = 4
    return pl.pallas_call(
        functools.partial(rescale, pieces),
        out_shape=jax.ShapeDtypeStruct((rows, channels), BF16),
        in_specs=[hbm] * 3,
        out_specs=hbm,
        scratch_shapes=[
            pltpu.VMEM((rows, channels), F32),
            pltpu.VMEM((rows, LANES), F32),
            pltpu.VMEM((1, channels), F32),
            pltpu.VMEM((rows, channels), BF16),
            sems((2,)),
            sems((pieces,)),
            sems((pieces,)),
        ],
        compiler_params=pltpu.CompilerParams(vmem_limit_bytes=VMEM_BYTES),
        cost_estimate=pl.CostEstimate(
            flops=2 * rows * channels, bytes_accessed=6 * rows * channels, transcendentals=0
        ),
    )(gated, scale, norm_gain[None, :])


def solution(mesh):
    placed = (P("ctx", "ch"), P("ctx", "ch"), P("ctx", "ch"), P("ctx", "ch"), P("ch"), P("ch"), P())
    return jax.shard_map(
        functools.partial(body, mesh),
        mesh=mesh,
        in_specs=placed,
        out_specs=P("ctx", "ch"),
        check_vma=False,
    )
```

```python
import functools

import jax
import jax.numpy as jnp
from jax import lax
from jax.experimental import pallas as pl
from jax.experimental.pallas import tpu as pltpu
from jax.sharding import PartitionSpec as P

MESH = pl.DeviceIdType.MESH
LANES = 128
VMEM_BYTES = 1013 * 64 * 1024
STRIP = 8
F32 = jnp.float32
BF16 = jnp.bfloat16


class Plan:
    def __init__(self, mesh, channels, filters, rows):
        self.blocks = mesh.shape["ctx"]
        self.halves = mesh.shape["ch"]
        self.rows = rows
        self.channels = channels
        self.filters = filters
        self.group = channels // filters
        self.each = max(1, filters // self.blocks)
        self.workers = filters // self.each
        self.share = self.each * self.group
        self.parts = 2 if self.each % 2 == 0 else 1
        self.each_part = self.each // self.parts
        self.share_part = self.share // self.parts
        self.span = channels // self.parts


def kernel(plan, pairs, query, key, value, taps, bias, gated_out, scale, *scratch):
    blocks, rows, group, span = plan.blocks, plan.rows, plan.group, plan.span
    part_rows = plan.share_part
    parts = range(plan.parts)
    scratch = list(scratch)
    take = lambda count: [scratch.pop(0) for _ in range(count)]
    pairs_here, table, table_here, query_here, key_here, value_here, taps_here, bias_here = take(8)
    (gated,) = take(1)
    flipped, taps_rows, taps_flipped, taps_got, toeplitz, total, results, squares = take(8)
    got, ordered, made, staged = (take(plan.parts) for _ in range(4))
    taps_send, taps_recv, square_send, square_recv, loaded, loaded_part, stored = take(7)
    go_send, go_recv, back_send, back_recv = take(4)

    me = lax.axis_index("ctx")
    half = lax.axis_index("ch")

    def only_worker(index):
        if plan.workers == blocks:
            return lambda fn: fn()
        return pl.when(index < plan.workers)

    def slot_of(step):
        return lax.rem(me + step, blocks)

    bits = [1 << place for place in range((blocks - 1).bit_length())]
    digits = [lax.rem(lax.div(me, bit), 2) for bit in bits]

    def peer_of(mask):
        peer = me
        for bit, digit in zip(bits, digits):
            flip = (mask // bit) % 2 if isinstance(mask, int) else lax.rem(lax.div(mask, bit), 2)
            peer = peer + flip * bit * (1 - 2 * digit)
        return peer

    near = [peer_of(blocks - step) for step in range(1, blocks)] if blocks <= 16 else None

    def each_peer(act):
        if near is not None:
            for peer in near:
                act(peer)
        else:
            pl.loop(1, blocks)(lambda step: act(peer_of(blocks - step)))

    def spread(count, act):
        if count <= 16:
            for index in range(count):
                act(index)
        else:
            pl.loop(0, count)(act)

    def column_copies(part):
        at = pl.ds(part * span, span)
        return [
            pltpu.make_async_copy(there.at[:, at], here.at[:, at], loaded_part.at[part, place])
            for place, (there, here) in enumerate(((key, key_here), (value, value_here)))
        ]

    def gated_store(part):
        at = pl.ds(part * span, span)
        return pltpu.make_async_copy(gated.at[:, at], gated_out.at[:, at], stored.at[part])

    whole_copies = [
        pltpu.make_async_copy(there, here, loaded.at[place])
        for place, (there, here) in enumerate(
            ((taps, taps_here), (pairs, pairs_here), (bias, bias_here), (query, query_here))
        )
    ]
    taps_load, pairs_load, bias_load, query_load = whole_copies
    table_load = pltpu.make_async_copy(table, table_here, loaded.at[4])

    strip = taps_flipped.shape[0] // plan.workers

    def strip_of(index):
        return pl.ds(pl.multiple_of(index * strip, strip), strip)

    def arrived(ref, sem):
        pltpu.make_async_remote_copy(
            src_ref=ref,
            dst_ref=ref,
            send_sem=sem,
            recv_sem=sem,
            device_id={"ctx": slot_of(1)},
            device_id_type=MESH,
        ).wait_recv()

    def from_others(wait):
        if plan.workers == blocks:
            wait(blocks - 1)
        else:
            pl.when(me < plan.workers)(lambda: wait(plan.workers - 1))
            pl.when(me >= plan.workers)(lambda: wait(plan.workers))

    def taps_copy(peer, slot):
        return pltpu.make_async_remote_copy(
            src_ref=taps_flipped.at[strip_of(peer)],
            dst_ref=taps_got.at[strip_of(slot)],
            send_sem=taps_send.at[0],
            recv_sem=taps_recv.at[0],
            device_id={"ctx": peer},
            device_id_type=MESH,
        )

    def go_copy(part, peer, slot):
        first = pl.multiple_of(part * span + peer * part_rows, group)
        return pltpu.make_async_remote_copy(
            src_ref=flipped.at[pl.ds(first, part_rows)],
            dst_ref=got[part].at[slot],
            send_sem=go_send.at[part],
            recv_sem=go_recv.at[part],
            device_id={"ctx": peer},
            device_id_type=MESH,
        )

    def back_copy(part, peer, slot):
        first = pl.multiple_of(part * span + slot * part_rows, group)
        return pltpu.make_async_remote_copy(
            src_ref=staged[part].at[peer],
            dst_ref=results.at[pl.ds(first, part_rows)],
            send_sem=back_send.at[part],
            recv_sem=back_recv.at[part],
            device_id={"ctx": peer},
            device_id_type=MESH,
        )

    def square_copy(peer, slot):
        return pltpu.make_async_remote_copy(
            src_ref=squares.at[half],
            dst_ref=squares.at[slot],
            send_sem=square_send.at[peer],
            recv_sem=square_recv.at[slot],
            device_id={"ch": peer},
            device_id_type=MESH,
        )

    barrier = pltpu.get_barrier_semaphore()

    @each_peer
    def _(peer):
        pl.semaphore_signal(barrier, inc=1, device_id={"ctx": peer}, device_id_type=MESH)

    for step in range(1, plan.halves):
        pl.semaphore_signal(
            barrier,
            inc=1,
            device_id={"ch": lax.rem(half + step, plan.halves)},
            device_id_type=MESH,
        )

    taps_load.start()
    for part in parts:
        for copy in column_copies(part):
            copy.start()
    for copy in (pairs_load, bias_load, query_load):
        copy.start()

    taps_load.wait()
    taps_rows[...] = jnp.transpose(taps_here[...])

    for part in parts:
        for index in range(plan.each_part):
            row = part * (plan.filters // plan.parts) + index
            taps_flipped[pl.ds(part * plan.each_part + index, plan.workers, stride=strip), :] = (
                taps_rows[pl.ds(row, plan.workers, stride=plan.each_part), :]
            )

    def signal_tile(columns):
        return key_here[:, columns].astype(F32) * value_here[:, columns].astype(F32)

    part_tiles = span // LANES

    for part in parts:
        for copy in column_copies(part):
            copy.wait()

        for tile in range(part * part_tiles, (part + 1) * part_tiles):
            at = pl.ds(tile * LANES, LANES)
            flipped[at, :] = jnp.transpose(signal_tile(at)).astype(BF16)

        if part == 0:
            pl.semaphore_wait(barrier, blocks - 1 + plan.halves - 1)

            @each_peer
            def _(peer):
                @only_worker(peer)
                def _():
                    taps_copy(peer, me).start()

        @each_peer
        def _(peer, part=part):
            @only_worker(peer)
            def _():
                go_copy(part, peer, me).start()

    pairs_load.wait()
    source, target, runner = (pairs_here[place : place + 1, :] for place in range(3))
    slots = lax.broadcasted_iota(jnp.int32, (blocks, pairs_here.shape[1]), 0)
    diagonal = source == target
    device_of = jnp.where(diagonal & (source == slots), runner, 0)
    holder = jnp.where(diagonal & (runner == slots), source, 0)
    for place, found in enumerate((device_of, holder)):
        table[place * blocks : (place + 1) * blocks, :] = jnp.broadcast_to(
            jnp.sum(found, axis=1, keepdims=True), (blocks, LANES)
        )
    table_load.start()

    ahead = lax.broadcasted_iota(jnp.int32, (rows, LANES), 1) >= lax.broadcasted_iota(
        jnp.int32, (rows, LANES), 0
    )
    run = 8

    def spread_taps(part):
        @pl.loop(part * plan.each_part, (part + 1) * plan.each_part)
        def _(index):
            def some(step, before):
                for block in [step * run + place for place in range(run)]:
                    line = taps_got[pl.ds(block * strip + index, 1), :]
                    turned = pltpu.roll(
                        jnp.broadcast_to(line, (rows, LANES)), 0, 1, stride=1, stride_axis=0
                    )
                    at = pl.ds(pl.multiple_of(block * LANES, LANES), LANES)
                    toeplitz[index, :, at] = jnp.where(ahead, turned, before).astype(BF16)
                    before = turned
                return before

            lax.fori_loop(0, blocks // run, some, jnp.zeros((rows, LANES), F32))

    @only_worker(me)
    def _():
        taps_got[strip_of(me), :] = taps_flipped[strip_of(me), :]
        for part in parts:
            first = pl.multiple_of(part * span + me * part_rows, group)
            got[part][me] = flipped[pl.ds(first, part_rows), :]

        arrived(taps_got.at[pl.ds(0, (blocks - 1) * strip)], taps_recv.at[0])
        for part in parts:
            spread_taps(part)

    table_load.wait()

    @only_worker(me)
    def _():
        for part in parts:
            arrived(got[part].at[pl.ds(0, blocks - 1)], go_recv.at[part])

            def in_order(block, part=part):
                piece = got[part][table_here[block, 0]]
                at = pl.ds(block * group, group)
                for index in range(plan.each_part):
                    ordered[part][index, at, :] = piece[index * group : (index + 1) * group]

            spread(blocks, in_order)

            @pl.loop(0, plan.each_part)
            def _(index, part=part):
                for pair in range(blocks // 2):
                    height = (blocks - 2 * pair) * group
                    product = jnp.dot(
                        ordered[part][index, :height, :],
                        toeplitz[
                            part * plan.each_part + index,
                            :,
                            2 * pair * LANES : 2 * (pair + 1) * LANES,
                        ],
                        preferred_element_type=F32,
                    )
                    even, odd = 2 * pair * group, (2 * pair + 1) * group
                    if pair == 0:
                        total[...] = product[:, :LANES]
                    else:
                        total[even:, :] += product[:, :LANES]
                    total[odd:, :] += product[: height - group, LANES:]
                at = pl.ds(pl.multiple_of(index * group, group), group)
                made[part][:, at, :] = total[...].astype(BF16).reshape(blocks, group, LANES)

            @each_peer
            def _(peer, part=part):
                staged[part][peer] = made[part][table_here[blocks + peer, 0]]
                back_copy(part, peer, me).start()

            first = pl.multiple_of(part * span + me * part_rows, group)
            results[pl.ds(first, part_rows), :] = made[part][table_here[blocks + me, 0]]

    bias_load.wait()
    query_load.wait()
    sums = jnp.zeros((rows, LANES), F32)
    for part in parts:

        from_others(
            lambda count, part=part: arrived(
                results.at[pl.ds(part * span, count * part_rows)], back_recv.at[part]
            )
        )

        for tile in range(part * part_tiles, (part + 1) * part_tiles):
            at = pl.ds(tile * LANES, LANES)
            conv = jnp.transpose(results[at, :].astype(F32))
            signal = signal_tile(at).astype(BF16).astype(F32)
            product = query_here[:, at].astype(F32) * (conv + bias_here[:, at] * signal)
            gated[:, at] = product
            sums = sums + product * product
        gated_store(part).start()

    squares[half] = jnp.broadcast_to(jnp.sum(sums, axis=1, keepdims=True), (rows, LANES))
    for step in range(1, plan.halves):
        square_copy(lax.rem(half + step, plan.halves), half).start()

    from_others(
        lambda count: arrived(taps_flipped.at[pl.ds(0, count * strip)], taps_send.at[0])
    )
    for part in parts:
        from_others(
            lambda count, part=part: arrived(
                flipped.at[pl.ds(part * span, count * part_rows)], go_send.at[part]
            )
        )

    @only_worker(me)
    def _():
        for part in parts:
            arrived(staged[part].at[pl.ds(0, blocks - 1)], back_send.at[part])

    for step in range(1, plan.halves):
        square_copy(half, lax.rem(half + step, plan.halves)).wait_recv()
    whole = squares[0]
    for other in range(1, plan.halves):
        whole = whole + squares[other]
    scale[...] = lax.rsqrt(whole / (plan.channels * plan.halves) + 1e-05)
    for part in parts:
        gated_store(part).wait()
    for step in range(1, plan.halves):
        square_copy(lax.rem(half + step, plan.halves), half).wait_send()


def rescale(pieces, gated, scale, gain, out, *scratch):
    gated_here, scale_here, gain_here, out_here, small, loaded, stored = scratch
    width = gated.shape[1] // pieces
    columns = [pl.ds(piece * width, width) for piece in range(pieces)]
    loads = [
        pltpu.make_async_copy(gated.at[:, at], gated_here.at[:, at], loaded.at[piece])
        for piece, at in enumerate(columns)
    ]
    stores = [
        pltpu.make_async_copy(out_here.at[:, at], out.at[:, at], stored.at[piece])
        for piece, at in enumerate(columns)
    ]
    scale_load = pltpu.make_async_copy(scale, scale_here, small.at[0])
    gain_load = pltpu.make_async_copy(gain, gain_here, small.at[1])
    for copy in [scale_load, gain_load] + loads:
        copy.start()
    scale_load.wait()
    gain_load.wait()
    for piece in range(pieces):
        loads[piece].wait()
        for first in range(piece * width, (piece + 1) * width, LANES):
            at = pl.ds(first, LANES)
            out_here[:, at] = (gated_here[:, at] * scale_here[...] * gain_here[:, at]).astype(BF16)
        stores[piece].start()
    for store in stores:
        store.wait()


def body(mesh, query, key, value, filter_taps, conv_bias, norm_gain, pair_list):
    rows, channels = query.shape
    plan = Plan(mesh, channels, filter_taps.shape[1], rows)
    blocks, parts = plan.blocks, plan.parts
    vmem = pl.BlockSpec(memory_space=pltpu.VMEM)
    hbm = pl.BlockSpec(memory_space=pltpu.HBM)
    strip = max(STRIP, plan.each)
    part_piece = (blocks, plan.share_part, LANES)
    sems = pltpu.SemaphoreType.DMA
    scratch = [
        pltpu.VMEM(pair_list.shape[::-1], jnp.int32),
        pltpu.VMEM((2 * blocks, LANES), jnp.int32),
        pltpu.SMEM((2 * blocks, LANES), jnp.int32),
        pltpu.VMEM((rows, channels), BF16),
        pltpu.VMEM((rows, channels), BF16),
        pltpu.VMEM((rows, channels), BF16),
        pltpu.VMEM(filter_taps.shape, F32),
        pltpu.VMEM((1, channels), F32),
        pltpu.VMEM((rows, channels), F32),
        pltpu.VMEM((channels, LANES), BF16),
        pltpu.VMEM((plan.filters, LANES), F32),
        pltpu.VMEM((plan.workers * strip, LANES), F32),
        pltpu.VMEM((blocks * strip, LANES), F32),
        pltpu.VMEM((plan.each, rows, blocks * LANES), BF16),
        pltpu.VMEM((blocks * plan.group, LANES), F32),
        pltpu.VMEM((channels, LANES), BF16),
        pltpu.VMEM((plan.halves, rows, LANES), F32),
    ]
    scratch += [pltpu.VMEM(part_piece, BF16)] * parts
    scratch += [pltpu.VMEM((plan.each_part, blocks * plan.group, LANES), BF16)] * parts
    scratch += [pltpu.VMEM(part_piece, BF16)] * parts
    scratch += [pltpu.VMEM(part_piece, BF16)] * parts
    scratch += [sems((1,)), sems((1,)), sems((plan.halves,)), sems((plan.halves,))]
    scratch += [sems((5,)), sems((parts, 2)), sems((parts,))]
    scratch += [sems((parts,))] * 4
    pairs = blocks * (blocks + 2) // 4
    gated, scale = pl.pallas_call(
        functools.partial(kernel, plan),
        out_shape=(
            jax.ShapeDtypeStruct((rows, channels), F32),
            jax.ShapeDtypeStruct((rows, LANES), F32),
        ),
        in_specs=[hbm] * 6,
        out_specs=(hbm, vmem),
        scratch_shapes=scratch,
        compiler_params=pltpu.CompilerParams(
            collective_id=0, has_side_effects=True, vmem_limit_bytes=VMEM_BYTES
        ),
        cost_estimate=pl.CostEstimate(
            flops=2 * plan.each * pairs * plan.group * rows * 2 * LANES,
            bytes_accessed=8 * rows * channels,
            transcendentals=0,
        ),
    )(pair_list.T, query, key, value, filter_taps, conv_bias[None, :])
    pieces = 4
    return pl.pallas_call(
        functools.partial(rescale, pieces),
        out_shape=jax.ShapeDtypeStruct((rows, channels), BF16),
        in_specs=[hbm] * 3,
        out_specs=hbm,
        scratch_shapes=[
            pltpu.VMEM((rows, channels), F32),
            pltpu.VMEM((rows, LANES), F32),
            pltpu.VMEM((1, channels), F32),
            pltpu.VMEM((rows, channels), BF16),
            sems((2,)),
            sems((pieces,)),
            sems((pieces,)),
        ],
        compiler_params=pltpu.CompilerParams(vmem_limit_bytes=VMEM_BYTES),
        cost_estimate=pl.CostEstimate(
            flops=2 * rows * channels, bytes_accessed=6 * rows * channels, transcendentals=0
        ),
    )(gated, scale, norm_gain[None, :])


def solution(mesh):
    placed = (P("ctx", "ch"), P("ctx", "ch"), P("ctx", "ch"), P("ctx", "ch"), P("ch"), P("ch"), P())
    return jax.shard_map(
        functools.partial(body, mesh),
        mesh=mesh,
        in_specs=placed,
        out_specs=P("ctx", "ch"),
        check_vma=False,
    )
```

```python
import functools

import jax
import jax.numpy as jnp
from jax import lax
from jax.experimental import pallas as pl
from jax.experimental.pallas import tpu as pltpu
from jax.sharding import PartitionSpec as P

MESH = pl.DeviceIdType.MESH
LANES = 128
VMEM_BYTES = 1013 * 64 * 1024
STRIP = 8
F32 = jnp.float32
BF16 = jnp.bfloat16


class Plan:
    def __init__(self, mesh, channels, filters, rows):
        self.blocks = mesh.shape["ctx"]
        self.halves = mesh.shape["ch"]
        self.rows = rows
        self.channels = channels
        self.filters = filters
        self.group = channels // filters
        self.each = max(1, filters // self.blocks)
        self.workers = filters // self.each
        self.share = self.each * self.group
        self.parts = 2 if self.each % 2 == 0 else 1
        self.each_part = self.each // self.parts
        self.share_part = self.share // self.parts
        self.span = channels // self.parts


def kernel(plan, pairs, query, key, value, taps, bias, gated_out, scale, *scratch):
    blocks, rows, group, span = plan.blocks, plan.rows, plan.group, plan.span
    part_rows = plan.share_part
    parts = range(plan.parts)
    scratch = list(scratch)
    take = lambda count: [scratch.pop(0) for _ in range(count)]
    pairs_here, table, table_here, query_here, key_here, value_here, taps_here, bias_here = take(8)
    (gated,) = take(1)
    flipped, taps_rows, taps_flipped, taps_got, toeplitz, total, results, squares = take(8)
    got, ordered, made, staged = (take(plan.parts) for _ in range(4))
    taps_send, taps_recv, square_send, square_recv, loaded, loaded_part, stored = take(7)
    go_send, go_recv, back_send, back_recv = take(4)

    me = lax.axis_index("ctx")
    half = lax.axis_index("ch")

    def only_worker(index):
        if plan.workers == blocks:
            return lambda fn: fn()
        return pl.when(index < plan.workers)

    def slot_of(step):
        return lax.rem(me + step, blocks)

    bits = [1 << place for place in range((blocks - 1).bit_length())]
    digits = [lax.rem(lax.div(me, bit), 2) for bit in bits]

    def peer_of(mask):
        peer = me
        for bit, digit in zip(bits, digits):
            flip = (mask // bit) % 2 if isinstance(mask, int) else lax.rem(lax.div(mask, bit), 2)
            peer = peer + flip * bit * (1 - 2 * digit)
        return peer

    near = [peer_of(blocks - step) for step in range(1, blocks)] if blocks <= 16 else None

    def each_peer(act):
        if near is not None:
            for peer in near:
                act(peer)
        else:
            pl.loop(1, blocks)(lambda step: act(peer_of(blocks - step)))

    def spread(count, act):
        if count <= 16:
            for index in range(count):
                act(index)
        else:
            pl.loop(0, count)(act)

    def column_copies(part):
        at = pl.ds(part * span, span)
        return [
            pltpu.make_async_copy(there.at[:, at], here.at[:, at], loaded_part.at[part, place])
            for place, (there, here) in enumerate(((key, key_here), (value, value_here)))
        ]

    def gated_store(piece):
        at = pl.ds(piece * (span // 4), span // 4)
        return pltpu.make_async_copy(gated.at[:, at], gated_out.at[:, at], stored.at[piece])

    whole_copies = [
        pltpu.make_async_copy(there, here, loaded.at[place])
        for place, (there, here) in enumerate(
            ((taps, taps_here), (pairs, pairs_here), (bias, bias_here), (query, query_here))
        )
    ]
    taps_load, pairs_load, bias_load, query_load = whole_copies
    table_load = pltpu.make_async_copy(table, table_here, loaded.at[4])

    strip = taps_flipped.shape[0] // plan.workers

    def strip_of(index):
        return pl.ds(pl.multiple_of(index * strip, strip), strip)

    def arrived(ref, sem):
        pltpu.make_async_remote_copy(
            src_ref=ref,
            dst_ref=ref,
            send_sem=sem,
            recv_sem=sem,
            device_id={"ctx": slot_of(1)},
            device_id_type=MESH,
        ).wait_recv()

    def from_others(wait):
        if plan.workers == blocks:
            wait(blocks - 1)
        else:
            pl.when(me < plan.workers)(lambda: wait(plan.workers - 1))
            pl.when(me >= plan.workers)(lambda: wait(plan.workers))

    def taps_copy(peer, slot):
        return pltpu.make_async_remote_copy(
            src_ref=taps_flipped.at[strip_of(peer)],
            dst_ref=taps_got.at[strip_of(slot)],
            send_sem=taps_send.at[0],
            recv_sem=taps_recv.at[0],
            device_id={"ctx": peer},
            device_id_type=MESH,
        )

    def go_copy(part, peer, slot):
        first = pl.multiple_of(part * span + peer * part_rows, group)
        return pltpu.make_async_remote_copy(
            src_ref=flipped.at[pl.ds(first, part_rows)],
            dst_ref=got[part].at[slot],
            send_sem=go_send.at[part],
            recv_sem=go_recv.at[part],
            device_id={"ctx": peer},
            device_id_type=MESH,
        )

    def back_copy(part, peer, slot):
        first = pl.multiple_of(part * span + slot * part_rows, group)
        return pltpu.make_async_remote_copy(
            src_ref=staged[part].at[peer],
            dst_ref=results.at[pl.ds(first, part_rows)],
            send_sem=back_send.at[part],
            recv_sem=back_recv.at[part],
            device_id={"ctx": peer},
            device_id_type=MESH,
        )

    def square_copy(peer, slot):
        return pltpu.make_async_remote_copy(
            src_ref=squares.at[half],
            dst_ref=squares.at[slot],
            send_sem=square_send.at[peer],
            recv_sem=square_recv.at[slot],
            device_id={"ch": peer},
            device_id_type=MESH,
        )

    barrier = pltpu.get_barrier_semaphore()

    @each_peer
    def _(peer):
        pl.semaphore_signal(barrier, inc=1, device_id={"ctx": peer}, device_id_type=MESH)

    for step in range(1, plan.halves):
        pl.semaphore_signal(
            barrier,
            inc=1,
            device_id={"ch": lax.rem(half + step, plan.halves)},
            device_id_type=MESH,
        )

    taps_load.start()
    for part in parts:
        for copy in column_copies(part):
            copy.start()
    for copy in (pairs_load, bias_load, query_load):
        copy.start()

    taps_load.wait()
    taps_rows[...] = jnp.transpose(taps_here[...])

    for part in parts:
        for index in range(plan.each_part):
            row = part * (plan.filters // plan.parts) + index
            taps_flipped[pl.ds(part * plan.each_part + index, plan.workers, stride=strip), :] = (
                taps_rows[pl.ds(row, plan.workers, stride=plan.each_part), :]
            )

    def signal_tile(columns):
        return key_here[:, columns].astype(F32) * value_here[:, columns].astype(F32)

    part_tiles = span // LANES

    for part in parts:
        for copy in column_copies(part):
            copy.wait()

        for tile in range(part * part_tiles, (part + 1) * part_tiles):
            at = pl.ds(tile * LANES, LANES)
            flipped[at, :] = jnp.transpose(signal_tile(at)).astype(BF16)

        if part == 0:
            pl.semaphore_wait(barrier, blocks - 1 + plan.halves - 1)

            @each_peer
            def _(peer):
                @only_worker(peer)
                def _():
                    taps_copy(peer, me).start()

        @each_peer
        def _(peer, part=part):
            @only_worker(peer)
            def _():
                go_copy(part, peer, me).start()

    pairs_load.wait()
    source, target, runner = (pairs_here[place : place + 1, :] for place in range(3))
    slots = lax.broadcasted_iota(jnp.int32, (blocks, pairs_here.shape[1]), 0)
    diagonal = source == target
    device_of = jnp.where(diagonal & (source == slots), runner, 0)
    holder = jnp.where(diagonal & (runner == slots), source, 0)
    for place, found in enumerate((device_of, holder)):
        table[place * blocks : (place + 1) * blocks, :] = jnp.broadcast_to(
            jnp.sum(found, axis=1, keepdims=True), (blocks, LANES)
        )
    table_load.start()

    ahead = lax.broadcasted_iota(jnp.int32, (rows, LANES), 1) >= lax.broadcasted_iota(
        jnp.int32, (rows, LANES), 0
    )
    run = 8

    def spread_taps(part):
        @pl.loop(part * plan.each_part, (part + 1) * plan.each_part)
        def _(index):
            def some(step, before):
                for block in [step * run + place for place in range(run)]:
                    line = taps_got[pl.ds(block * strip + index, 1), :]
                    turned = pltpu.roll(
                        jnp.broadcast_to(line, (rows, LANES)), 0, 1, stride=1, stride_axis=0
                    )
                    at = pl.ds(pl.multiple_of(block * LANES, LANES), LANES)
                    toeplitz[index, :, at] = jnp.where(ahead, turned, before).astype(BF16)
                    before = turned
                return before

            lax.fori_loop(0, blocks // run, some, jnp.zeros((rows, LANES), F32))

    @only_worker(me)
    def _():
        taps_got[strip_of(me), :] = taps_flipped[strip_of(me), :]
        for part in parts:
            first = pl.multiple_of(part * span + me * part_rows, group)
            got[part][me] = flipped[pl.ds(first, part_rows), :]

        arrived(taps_got.at[pl.ds(0, (blocks - 1) * strip)], taps_recv.at[0])
        for part in parts:
            spread_taps(part)

    table_load.wait()

    @only_worker(me)
    def _():
        for part in parts:
            arrived(got[part].at[pl.ds(0, blocks - 1)], go_recv.at[part])

            def in_order(block, part=part):
                piece = got[part][table_here[block, 0]]
                at = pl.ds(block * group, group)
                for index in range(plan.each_part):
                    ordered[part][index, at, :] = piece[index * group : (index + 1) * group]

            spread(blocks, in_order)

            @pl.loop(0, plan.each_part)
            def _(index, part=part):
                for pair in range(blocks // 2):
                    height = (blocks - 2 * pair) * group
                    product = jnp.dot(
                        ordered[part][index, :height, :],
                        toeplitz[
                            part * plan.each_part + index,
                            :,
                            2 * pair * LANES : 2 * (pair + 1) * LANES,
                        ],
                        preferred_element_type=F32,
                    )
                    even, odd = 2 * pair * group, (2 * pair + 1) * group
                    if pair == 0:
                        total[...] = product[:, :LANES]
                    else:
                        total[even:, :] += product[:, :LANES]
                    total[odd:, :] += product[: height - group, LANES:]
                at = pl.ds(pl.multiple_of(index * group, group), group)
                made[part][:, at, :] = total[...].astype(BF16).reshape(blocks, group, LANES)

            @each_peer
            def _(peer, part=part):
                staged[part][peer] = made[part][table_here[blocks + peer, 0]]
                back_copy(part, peer, me).start()

            first = pl.multiple_of(part * span + me * part_rows, group)
            results[pl.ds(first, part_rows), :] = made[part][table_here[blocks + me, 0]]

    bias_load.wait()
    query_load.wait()
    sums = jnp.zeros((rows, LANES), F32)
    for part in parts:

        from_others(
            lambda count, part=part: arrived(
                results.at[pl.ds(part * span, count * part_rows)], back_recv.at[part]
            )
        )

        for tile in range(part * part_tiles, (part + 1) * part_tiles):
            at = pl.ds(tile * LANES, LANES)
            conv = jnp.transpose(results[at, :].astype(F32))
            signal = signal_tile(at).astype(BF16).astype(F32)
            product = query_here[:, at].astype(F32) * (conv + bias_here[:, at] * signal)
            gated[:, at] = product
            sums = sums + product * product
            if (tile + 1) % (part_tiles // 4) == 0:
                gated_store(tile // (part_tiles // 4)).start()

    squares[half] = jnp.broadcast_to(jnp.sum(sums, axis=1, keepdims=True), (rows, LANES))
    for step in range(1, plan.halves):
        square_copy(lax.rem(half + step, plan.halves), half).start()

    from_others(
        lambda count: arrived(taps_flipped.at[pl.ds(0, count * strip)], taps_send.at[0])
    )
    for part in parts:
        from_others(
            lambda count, part=part: arrived(
                flipped.at[pl.ds(part * span, count * part_rows)], go_send.at[part]
            )
        )

    @only_worker(me)
    def _():
        for part in parts:
            arrived(staged[part].at[pl.ds(0, blocks - 1)], back_send.at[part])

    for step in range(1, plan.halves):
        square_copy(half, lax.rem(half + step, plan.halves)).wait_recv()
    whole = squares[0]
    for other in range(1, plan.halves):
        whole = whole + squares[other]
    scale[...] = lax.rsqrt(whole / (plan.channels * plan.halves) + 1e-05)
    for piece in range(4 * plan.parts):
        gated_store(piece).wait()
    for step in range(1, plan.halves):
        square_copy(lax.rem(half + step, plan.halves), half).wait_send()


def rescale(pieces, gated, scale, gain, out, *scratch):
    gated_here, scale_here, gain_here, out_here, small, loaded, stored = scratch
    width = gated.shape[1] // pieces
    columns = [pl.ds(piece * width, width) for piece in range(pieces)]
    loads = [
        pltpu.make_async_copy(gated.at[:, at], gated_here.at[:, at], loaded.at[piece])
        for piece, at in enumerate(columns)
    ]
    stores = [
        pltpu.make_async_copy(out_here.at[:, at], out.at[:, at], stored.at[piece])
        for piece, at in enumerate(columns)
    ]
    scale_load = pltpu.make_async_copy(scale, scale_here, small.at[0])
    gain_load = pltpu.make_async_copy(gain, gain_here, small.at[1])
    for copy in [scale_load, gain_load] + loads:
        copy.start()
    scale_load.wait()
    gain_load.wait()
    for piece in range(pieces):
        loads[piece].wait()
        for first in range(piece * width, (piece + 1) * width, LANES):
            at = pl.ds(first, LANES)
            out_here[:, at] = (gated_here[:, at] * scale_here[...] * gain_here[:, at]).astype(BF16)
        stores[piece].start()
    for store in stores:
        store.wait()


def body(mesh, query, key, value, filter_taps, conv_bias, norm_gain, pair_list):
    rows, channels = query.shape
    plan = Plan(mesh, channels, filter_taps.shape[1], rows)
    blocks, parts = plan.blocks, plan.parts
    vmem = pl.BlockSpec(memory_space=pltpu.VMEM)
    hbm = pl.BlockSpec(memory_space=pltpu.HBM)
    strip = max(STRIP, plan.each)
    part_piece = (blocks, plan.share_part, LANES)
    sems = pltpu.SemaphoreType.DMA
    scratch = [
        pltpu.VMEM(pair_list.shape[::-1], jnp.int32),
        pltpu.VMEM((2 * blocks, LANES), jnp.int32),
        pltpu.SMEM((2 * blocks, LANES), jnp.int32),
        pltpu.VMEM((rows, channels), BF16),
        pltpu.VMEM((rows, channels), BF16),
        pltpu.VMEM((rows, channels), BF16),
        pltpu.VMEM(filter_taps.shape, F32),
        pltpu.VMEM((1, channels), F32),
        pltpu.VMEM((rows, channels), F32),
        pltpu.VMEM((channels, LANES), BF16),
        pltpu.VMEM((plan.filters, LANES), F32),
        pltpu.VMEM((plan.workers * strip, LANES), F32),
        pltpu.VMEM((blocks * strip, LANES), F32),
        pltpu.VMEM((plan.each, rows, blocks * LANES), BF16),
        pltpu.VMEM((blocks * plan.group, LANES), F32),
        pltpu.VMEM((channels, LANES), BF16),
        pltpu.VMEM((plan.halves, rows, LANES), F32),
    ]
    scratch += [pltpu.VMEM(part_piece, BF16)] * parts
    scratch += [pltpu.VMEM((plan.each_part, blocks * plan.group, LANES), BF16)] * parts
    scratch += [pltpu.VMEM(part_piece, BF16)] * parts
    scratch += [pltpu.VMEM(part_piece, BF16)] * parts
    scratch += [sems((1,)), sems((1,)), sems((plan.halves,)), sems((plan.halves,))]
    scratch += [sems((5,)), sems((parts, 2)), sems((4 * parts,))]
    scratch += [sems((parts,))] * 4
    pairs = blocks * (blocks + 2) // 4
    gated, scale = pl.pallas_call(
        functools.partial(kernel, plan),
        out_shape=(
            jax.ShapeDtypeStruct((rows, channels), F32),
            jax.ShapeDtypeStruct((rows, LANES), F32),
        ),
        in_specs=[hbm] * 6,
        out_specs=(hbm, vmem),
        scratch_shapes=scratch,
        compiler_params=pltpu.CompilerParams(
            collective_id=0, has_side_effects=True, vmem_limit_bytes=VMEM_BYTES
        ),
        cost_estimate=pl.CostEstimate(
            flops=2 * plan.each * pairs * plan.group * rows * 2 * LANES,
            bytes_accessed=8 * rows * channels,
            transcendentals=0,
        ),
    )(pair_list.T, query, key, value, filter_taps, conv_bias[None, :])
    pieces = 4
    return pl.pallas_call(
        functools.partial(rescale, pieces),
        out_shape=jax.ShapeDtypeStruct((rows, channels), BF16),
        in_specs=[hbm] * 3,
        out_specs=hbm,
        scratch_shapes=[
            pltpu.VMEM((rows, channels), F32),
            pltpu.VMEM((rows, LANES), F32),
            pltpu.VMEM((1, channels), F32),
            pltpu.VMEM((rows, channels), BF16),
            sems((2,)),
            sems((pieces,)),
            sems((pieces,)),
        ],
        compiler_params=pltpu.CompilerParams(vmem_limit_bytes=VMEM_BYTES),
        cost_estimate=pl.CostEstimate(
            flops=2 * rows * channels, bytes_accessed=6 * rows * channels, transcendentals=0
        ),
    )(gated, scale, norm_gain[None, :])


def solution(mesh):
    placed = (P("ctx", "ch"), P("ctx", "ch"), P("ctx", "ch"), P("ctx", "ch"), P("ch"), P("ch"), P())
    return jax.shard_map(
        functools.partial(body, mesh),
        mesh=mesh,
        in_specs=placed,
        out_specs=P("ctx", "ch"),
        check_vma=False,
    )
```
